256 devices in a mesh: gx: 32 (over x, z), gz: 8 (over y, core).
Axes of the slice: x: 4, y: 4, z: 8, core: 2. Of those that a mesh axis runs over, the one named last changes fastest.
Arguments:
- potential: float32 [32, 2048, 2048], P('gz', 'gx'), may hold values from -6 to 6
- regions: int32 [32, 2048, 2048], P('gz', 'gx'), may hold values from 0 to 15, as said below
- charge: float32 [32, 2048, 2048], P('gz', 'gx'), may hold values from -6 to 6
- levels: float32 [16], replicated, may hold values from -2 to 2
Outputs:
- field_out: float32 [32, 2048, 2048], P('gz', 'gx')
- multipoles: float32 [32, 64], P('gz', 'gx')
The draws below stay inside these ranges and needn't reach their ends.
Inputs may be any that keep to these rules, and one draw needn't show every extreme that they name: `regions`: about three quarters of the cells are free space (id 0); the others carry ids 1 to 15 evenly.
All inputs are finite; a program needn't handle non-finite values.
Results may differ from the reference program's by a relative error of at most 0.00026.
Values sent between devices are 32-bit elements; how exact they have to be, the bound alone decides.
No kernel may reach another device: no remote copies, remote signals or barrier semaphores. Data moves between devices by JAX's collectives and lax.ppermute only.
A program may use at most 128 MiB of HBM per device.

```python
import jax
import jax.numpy as jnp
from jax import lax

NY = 2048
K = 64
NREG = 16
SWEEPS = 4
NX = 2048
NZ = 32


def draw_regions(key, part):
    key = jax.random.fold_in(key, 7)
    picks = jax.random.randint(key, (NZ, NX, NY), 0, 4 * (NREG - 1))
    return jnp.where(picks < 3 * (NREG - 1), 0, picks - 3 * (NREG - 1) + 1).astype(jnp.int32)


def shard_levels(stream_key, shape, split, least, high):
    def one(axis_at, blocks):
        draws = jax.random.uniform(jax.random.fold_in(jax.random.fold_in(stream_key, 6), axis_at), (blocks,), jnp.float32, least / len(split), high / len(split))
        return jnp.repeat(jnp.exp(draws), shape[axis_at] // blocks).reshape((-1,) + (1,) * (len(shape) - axis_at - 1))

    factor_of = one(*split[0])
    for cut in split[1:]:
        factor_of = factor_of * one(*cut)
    return factor_of


def scatter_about(stream_key, extent, width, limit, shards=(), held_as=jnp.bfloat16):
    values = width * jax.random.normal(stream_key, extent, jnp.float32)
    if shards:
        values = values * shard_levels(stream_key, extent, shards, -0.22, 0.18)
    return jnp.clip(values, -limit, limit).astype(held_as)


def setup_inputs(seed: int = 0) -> dict:
    keys = jax.random.split(jax.random.key(seed), 5)
    return {
        "potential": scatter_about(keys[0], (NZ, NX, NY), 1.0, 6.0, ((0, 8), (1, 32)), jnp.float32),
        "regions": draw_regions(jax.random.fold_in(keys[4], 71), 0),
        "charge": scatter_about(keys[2], (NZ, NX, NY), 1.0, 6.0, ((0, 8), (1, 32)), jnp.float32),
        "levels": jnp.clip(jax.random.uniform(keys[3], (NREG,), jnp.float32, -2.0, 2.0), -2.0, 2.0),
    }


relax_factor = 1.5

def parity_grid(z_start, x_start, planes, row_count, columns):
    shape = (planes, row_count, columns)
    total = lax.broadcasted_iota(jnp.int32, shape, 0) + lax.broadcasted_iota(jnp.int32, shape, 1) + lax.broadcasted_iota(jnp.int32, shape, 2)
    return (total + z_start + x_start + 8) % 2

def relax_cells(values, free_cells, charge_in, parity_in, colour):
    center = values[1:-1, 1:-1]
    side_pad = jnp.pad(center, ((0, 0), (0, 0), (1, 1)))
    beside = values[2:, 1:-1] + values[:-2, 1:-1] + values[1:-1, 2:] + values[1:-1, :-2] + side_pad[:, :, 2:] + side_pad[:, :, :-2]
    target = (beside + charge_in) / 6.0
    moved = center + relax_factor * (target - center)
    return jnp.where((free_cells > 0.5) & (parity_in == colour), moved, center)

def make_basis(x_start, row_count, rows_total, columns, terms):
    row_pos = (x_start + jnp.arange(row_count, dtype=jnp.int32)).astype(jnp.float32)
    col_pos = jnp.arange(columns, dtype=jnp.int32).astype(jnp.float32)
    coord_x = (row_pos + 0.5) * (2.0 / rows_total) - 1.0
    coord_y = (col_pos + 0.5) * (2.0 / columns) - 1.0
    coord_x = coord_x[:, None] + 0.0 * coord_y[None, :]
    coord_y = coord_y[None, :] + 0.0 * coord_x
    radius = jnp.sqrt(coord_x * coord_x + coord_y * coord_y)
    angle_grid = jnp.arctan2(coord_y, coord_x)
    orders = jnp.arange(1, terms // 2 + 1, dtype=jnp.int32).astype(jnp.float32)[:, None, None]
    return jnp.concatenate([radius * jnp.cos(orders * angle_grid), radius * jnp.sin(orders * angle_grid)], axis=0)

def reference(potential, regions, charge, levels):
    free_cells = (regions == 0).astype(jnp.float32)
    field_now = jnp.where(free_cells > 0.5, potential, levels[regions]).astype(jnp.float32)
    parity_in = parity_grid(0, 0, NZ, NX, NY)
    for sweep_index in range(SWEEPS):
        for colour in (0, 1):
            padded = jnp.pad(field_now, ((1, 1), (1, 1), (0, 0)))
            field_now = relax_cells(padded, free_cells, charge, parity_in, colour)
    block = min(64, NX)
    summed = jnp.zeros((NZ, K), jnp.float32)
    for start in range(0, NX, block):
        basis_table = make_basis(start, block, NX, NY, K)
        summed = summed + jnp.einsum('zxy,kxy->zk', field_now[:, start:start + block], basis_table, precision=lax.Precision.HIGHEST)
    multipoles = summed * (1.0 / jnp.sqrt(jnp.float32(NX) * jnp.float32(NY)))
    return (field_now, multipoles)
```

```python
import functools

import jax
import jax.numpy as jnp
from jax import lax
from jax.experimental import pallas as pl
from jax.experimental.pallas import tpu as pltpu
from jax.sharding import PartitionSpec as P

K = 64
SWEEPS = 4
HALF = K // 2
PINNED = 1e30
VMEM_BYTES = 40 * 1024 * 1024


def vmem():
    return pl.BlockSpec(memory_space=pltpu.VMEM)


def smem():
    return pl.BlockSpec(memory_space=pltpu.SMEM)


def column_parity(rows, columns):
    return lax.broadcasted_iota(jnp.int32, (rows, columns), 1) % 2


def pack_kernel(pot_ref, reg_ref, chg_ref, lev_ref, f0_ref, f1_ref, c0_ref, c1_ref, field, charge):
    plane = pl.program_id(0)
    rows, columns = f0_ref.shape[1:]
    table = jnp.broadcast_to(lev_ref[...], (8, 128))
    even = column_parity(rows, 128) == plane % 2
    for c in range(columns // 128):
        at = pl.ds(128 * c, 128)
        for j in range(0, 2 * rows, 8):
            to = pl.ds(j, 8)
            region = reg_ref[0, to, at]
            pinned = jnp.take_along_axis(table, region, axis=1)
            free = region == 0
            field[c, to, :] = jnp.where(free, pot_ref[0, to, at], pinned)
            charge[c, to, :] = jnp.where(free, chg_ref[0, to, at], PINNED)
        for source, out0, out1 in ((field, f0_ref, f1_ref), (charge, c0_ref, c1_ref)):
            a = source[c, pl.ds(0, rows, stride=2), :]
            b = source[c, pl.ds(1, rows, stride=2), :]
            out0[0, :, at] = jnp.where(even, a, b)
            out1[0, :, at] = jnp.where(even, b, a)


def pack(potential, regions, charge, levels):
    planes, rows, columns = potential.shape
    table = jnp.pad(levels, (0, 128 - levels.shape[0]))[None, :]
    whole = pl.BlockSpec((1, rows, columns), lambda z: (z, 0, 0))
    half = pl.BlockSpec((1, rows // 2, columns), lambda z: (z, 0, 0))
    out = jax.ShapeDtypeStruct((planes, rows // 2, columns), jnp.float32)
    return pl.pallas_call(
        pack_kernel,
        grid=(planes,),
        in_specs=[whole, whole, whole, pl.BlockSpec((1, 128), lambda z: (0, 0))],
        out_specs=[half] * 4,
        out_shape=[out] * 4,
        scratch_shapes=[pltpu.VMEM((columns // 128, rows, 128), jnp.float32)] * 2,
        compiler_params=pltpu.CompilerParams(vmem_limit_bytes=VMEM_BYTES),
        name="pack",
    )(potential, regions, charge, table)


def merge_rows(top, planes, columns, keep):
    mask = column_parity(1, columns) == keep
    return jnp.concatenate([jnp.where(mask, top[z], top[z + 1]) for z in range(0, planes, 2)], axis=0)


def sends(read, planes, rows, columns, colour, core, odd, ze_ref, zi_ref, xe_ref, xo_ref):
    for j in range(0, rows, 8):
        low, high = read(0, j, 8), read(planes - 1, j, 8)
        ze_ref[pl.ds(j, 8), :] = jnp.where(core == 0, low, high)
        zi_ref[pl.ds(j, 8), :] = jnp.where(core == 0, high, low)
    last = [read(z, rows - 1, 1) for z in range(planes)]
    first = [read(z, 0, 1) for z in range(planes)]
    above = merge_rows(last, planes, columns, 1 - colour)
    below = merge_rows(first, planes, columns, colour)
    xe_ref[...] = jnp.where(odd == 0, above, below)
    xo_ref[...] = jnp.where(odd == 0, below, above)


def relax(where, own_ref, other_ref, charge_ref, ze_ref, zi_ref, xe_ref, xo_ref, colour, put):
    core, odd = where[0], where[1]
    ze_live, below_live, above_live = where[2], where[3], where[4]
    planes, rows, columns = own_ref.shape
    column = lax.broadcasted_iota(jnp.int32, (8, columns), 1)
    row = lax.broadcasted_iota(jnp.int32, (8, columns), 0)
    xe, xo = xe_ref[...], xo_ref[...]
    below = jnp.where(below_live == 1, jnp.where(odd == 0, xo, xe), 0.0)
    above = jnp.where(above_live == 1, jnp.where(odd == 0, xe, xo), 0.0)

    def outer(j):
        far = jnp.where(ze_live == 1, ze_ref[pl.ds(j, 8), :], 0.0)
        return far, zi_ref[pl.ds(j, 8), :]

    for z in range(planes):
        first_row = (column % 2) == (z + colour) % 2
        for j in range(0, rows, 8):
            at = pl.ds(j, 8)
            mid = other_ref[z, at, :]
            if z == 0:
                far, near = outer(j)
                z_low = jnp.where(core == 0, far, near)
            else:
                z_low = other_ref[z - 1, at, :]
            if z == planes - 1:
                far, near = outer(j)
                z_high = jnp.where(core == 0, near, far)
            else:
                z_high = other_ref[z + 1, at, :]
            edge_low = below[z // 2 : z // 2 + 1] if j == 0 else other_ref[z, pl.ds(j - 1, 1), :]
            edge_high = above[z // 2 : z // 2 + 1] if j + 8 == rows else other_ref[z, pl.ds(j + 8, 1), :]
            x_low = jnp.where(row == 0, jnp.broadcast_to(edge_low, mid.shape), pltpu.roll(mid, 1, 0))
            x_high = jnp.where(row == 7, jnp.broadcast_to(edge_high, mid.shape), pltpu.roll(mid, 7, 0))
            y_low = jnp.where(column == 0, 0.0, pltpu.roll(mid, 1, 1))
            y_high = jnp.where(column == columns - 1, 0.0, pltpu.roll(mid, columns - 1, 1))
            charge = charge_ref[z, at, :]
            beside = z_low + z_high + mid + jnp.where(first_row, x_low, x_high) + y_low + y_high
            own = own_ref[z, at, :]
            put(z, j, jnp.where(charge < PINNED, 0.25 * (beside + charge) - 0.5 * own, own))


def first_send_kernel(colour, where, field_ref, ze_out, zi_out, xe_out, xo_out):
    planes, rows, columns = field_ref.shape
    sends(lambda z, j, n: field_ref[z, pl.ds(j, n), :], planes, rows, columns, colour, where[0], where[1],
          ze_out, zi_out, xe_out, xo_out)


def relax_kernel(colour, where, own_ref, other_ref, charge_ref, ze_ref, zi_ref, xe_ref, xo_ref,
                 out_ref, ze_out, zi_out, xe_out, xo_out):
    planes, rows, columns = own_ref.shape

    def put(z, j, value):
        out_ref[z, pl.ds(j, 8), :] = value

    relax(where, own_ref, other_ref, charge_ref, ze_ref, zi_ref, xe_ref, xo_ref, colour, put)
    sends(lambda z, j, n: out_ref[z, pl.ds(j, n), :], planes, rows, columns, colour, where[0], where[1],
          ze_out, zi_out, xe_out, xo_out)


def last_kernel(where, own_ref, other_ref, charge_ref, ze_ref, zi_ref, xe_ref, xo_ref, field_ref, rows_ref):
    columns = own_ref.shape[2]

    def put(z, j, value):
        even = column_parity(8, columns) == z % 2
        zero = other_ref[z, pl.ds(j, 8), :]
        low, high = jnp.where(even, zero, value), jnp.where(even, value, zero)
        for c in range(columns // 128):
            at = slice(128 * c, 128 * c + 128)
            rows_ref[z, c, pl.ds(2 * j, 8, stride=2), :] = low[:, at]
            rows_ref[z, c, pl.ds(2 * j + 1, 8, stride=2), :] = high[:, at]
            field_ref[z, pl.ds(2 * j, 16), pl.ds(128 * c, 128)] = rows_ref[z, c, pl.ds(2 * j, 16), :]

    relax(where, own_ref, other_ref, charge_ref, ze_ref, zi_ref, xe_ref, xo_ref, 1, put)


def params():
    return pltpu.CompilerParams(vmem_limit_bytes=VMEM_BYTES)


def send_shapes(planes, rows, columns):
    side = jax.ShapeDtypeStruct((rows, columns), jnp.float32)
    line = jax.ShapeDtypeStruct((planes // 2, columns), jnp.float32)
    return [side, side, line, line]


def first_send(where, field, colour):
    return pl.pallas_call(
        functools.partial(first_send_kernel, colour),
        in_specs=[smem(), vmem()],
        out_specs=[vmem()] * 4,
        out_shape=send_shapes(*field.shape),
        compiler_params=params(),
        name="first_send",
    )(where, field)


def half_sweep(where, own, other, charge, halos, colour):
    return pl.pallas_call(
        functools.partial(relax_kernel, colour),
        in_specs=[smem()] + [vmem()] * 7,
        out_specs=[vmem()] * 5,
        out_shape=[jax.ShapeDtypeStruct(own.shape, jnp.float32)] + send_shapes(*own.shape),
        compiler_params=params(),
        name="relax",
    )(where, own, other, charge, *halos)


def last_half_sweep(where, own, other, charge, halos):
    planes, rows, columns = own.shape
    return pl.pallas_call(
        last_kernel,
        in_specs=[smem()] + [vmem()] * 7,
        out_specs=vmem(),
        out_shape=jax.ShapeDtypeStruct((planes, 2 * rows, columns), jnp.float32),
        scratch_shapes=[pltpu.VMEM((planes, columns // 128, 2 * rows, 128), jnp.float32)],
        compiler_params=params(),
        name="relax_last",
    )(where, own, other, charge, *halos)


def split(value):
    high = value.astype(jnp.bfloat16)
    return high, (value - high.astype(jnp.float32)).astype(jnp.bfloat16)


def multipole_kernel(rows_total, start_ref, field_ref, out_ref, left, right, total):
    step = pl.program_id(0)
    planes, _, columns = field_ref.shape
    turns = HALF // 2
    row = start_ref[0] + step * 8 + lax.broadcasted_iota(jnp.int32, (8, columns), 0)
    col = lax.broadcasted_iota(jnp.int32, (8, columns), 1)
    u = (row.astype(jnp.float32) + 0.5) * (2.0 / rows_total) - 1.0
    v = (col.astype(jnp.float32) + 0.5) * (2.0 / columns) - 1.0
    inverse = lax.rsqrt(u * u + v * v)
    c1, s1 = u * inverse, v * inverse
    c2, s2 = c1 * c1 - s1 * s1, 2.0 * (c1 * s1)

    def put(ref, index, count, value):
        high, low = split(value)
        ref[pl.ds(index * 8, 8), :] = high
        ref[pl.ds((count + index) * 8, 8), :] = low

    twice = 2.0 * c2
    count = 2 * turns
    c_old, s_old = jnp.ones_like(c2), jnp.zeros_like(c2)
    c_now, s_now = c2, s2
    put(left, 0, count, c_old)
    put(left, turns, count, s_old)
    for a in range(1, turns):
        put(left, a, count, c_now)
        put(left, turns + a, count, s_now)
        c_old, s_old, c_now, s_now = c_now, s_now, twice * c_now - c_old, twice * s_now - s_old
    radial = (u, v, u * c1 - v * s1, u * s1 + v * c1)
    for z in range(planes):
        f = field_ref[z]
        for m, weight in enumerate(radial):
            put(right, z * 4 + m, 4 * planes, f * weight)
    product = lax.dot_general(
        left[...], right[...], (((1,), (1,)), ((), ())), preferred_element_type=jnp.float32
    )

    @pl.when(step == 0)
    def _():
        total[...] = product

    @pl.when(step > 0)
    def _():
        total[...] += product

    @pl.when(step == pl.num_programs(0) - 1)
    def _():
        whole = total[...]
        n = 8 * count
        m = 32 * planes
        whole = (whole[:n, :m] + whole[n:, :m]) + (whole[:n, m:] + whole[n:, m:])
        i = lax.broadcasted_iota(jnp.int32, whole.shape, 0)
        k = lax.broadcasted_iota(jnp.int32, whole.shape, 1)
        whole = jnp.where(i % 8 == k % 8, whole, 0.0)
        out_ref[...] = jnp.sum(whole.reshape(count, 8, m), axis=1)


def multipole_sums(start, field, rows_total):
    planes, rows, columns = field.shape
    turns = HALF // 2
    table = pl.pallas_call(
        functools.partial(multipole_kernel, rows_total),
        grid=(rows // 8,),
        in_specs=[smem(), pl.BlockSpec((planes, 8, columns), lambda i: (0, i, 0))],
        out_specs=pl.BlockSpec((2 * turns, 32 * planes), lambda i: (0, 0)),
        out_shape=jax.ShapeDtypeStruct((2 * turns, 32 * planes), jnp.float32),
        scratch_shapes=[
            pltpu.VMEM((32 * turns, columns), jnp.bfloat16),
            pltpu.VMEM((64 * planes, columns), jnp.bfloat16),
            pltpu.VMEM((32 * turns, 64 * planes), jnp.float32),
        ],
        compiler_params=params(),
        name="multipole",
    )(start, field)
    table = table.reshape(2, turns, planes, 2, 2, 8).sum(-1)
    cos_part = table[0, ..., 0] - table[1, ..., 1]
    sin_part = table[1, ..., 0] + table[0, ..., 1]
    order = lambda t: jnp.transpose(t, (1, 0, 2)).reshape(planes, HALF)
    return jnp.concatenate([order(cos_part), order(sin_part)], axis=1)


def swaps(pairs):
    return [(a, b) for a, b in pairs] + [(b, a) for a, b in pairs]


def reduce_rows(part):
    if lax.axis_size("gx") != 32:
        return lax.psum(part, "gx")
    even = swaps([(8 * x + z, 8 * x + z + 1) for x in range(4) for z in (0, 2, 4, 6)])
    odd = swaps([(8 * x + z, 8 * x + (z + 1) % 8) for x in range(4) for z in (1, 3, 5, 7)])
    near = swaps([(z + 8 * x, z + 8 * x + 8) for z in range(8) for x in (0, 2)])
    far = swaps([(z + 8 * x, z + (8 * x + 8) % 32) for z in range(8) for x in (1, 3)])
    swap = lambda value, pairs: lax.ppermute(value, "gx", pairs)
    pair = part + swap(part, even)
    side = swap(pair, odd)
    across = swap(side, even)
    last = swap(across, odd)
    ring = (pair + last) + (side + across)
    ring = ring + swap(ring, near)
    return ring + swap(ring, far)


def local(potential, regions, charge, levels):
    planes, row_count, columns = potential.shape
    gx, gz = lax.axis_index("gx"), lax.axis_index("gz")
    nx, nz = lax.axis_size("gx"), lax.axis_size("gz")
    rows_total = nx * row_count
    core = gz % 2
    where = jnp.stack(
        [
            core,
            gx % 2,
            jnp.where(core == 0, gz > 0, gz < nz - 1).astype(jnp.int32),
            (gx > 0).astype(jnp.int32),
            (gx < nx - 1).astype(jnp.int32),
        ]
    ).astype(jnp.int32)
    z_far = swaps([(i, (i + 1) % nz) for i in range(1, nz, 2)])
    z_near = [(i, i ^ 1) for i in range(nz)]
    x_even = [(i, i ^ 1) for i in range(nx)]
    x_odd = swaps([(i, (i + 1) % nx) for i in range(1, nx, 2)])

    def exchange(ze, zi, xe, xo):
        return (
            lax.ppermute(ze, "gz", z_far),
            lax.ppermute(zi, "gz", z_near),
            lax.ppermute(xe, "gx", x_even),
            lax.ppermute(xo, "gx", x_odd),
        )

    zero, one, charge0, charge1 = pack(potential, regions, charge, levels)
    halos = exchange(*first_send(where, one, 1))
    for sweep in range(SWEEPS):
        zero, *out = half_sweep(where, zero, one, charge0, halos, 0)
        halos = exchange(*out)
        if sweep < SWEEPS - 1:
            one, *out = half_sweep(where, one, zero, charge1, halos, 1)
            halos = exchange(*out)
        else:
            field = last_half_sweep(where, one, zero, charge1, halos)
    start = (gx * row_count).astype(jnp.int32)[None]
    part = multipole_sums(start, field, rows_total)
    part = part * (1.0 / jnp.sqrt(jnp.float32(rows_total) * jnp.float32(columns)))
    summed = reduce_rows(part)
    share = K // nx
    return field, lax.dynamic_slice_in_dim(summed, gx * share, share, 1)


def solution(mesh):
    in_specs = (P("gz", "gx", None), P("gz", "gx", None), P("gz", "gx", None), P())
    out_specs = (P("gz", "gx", None), P("gz", "gx"))
    return jax.shard_map(local, mesh=mesh, in_specs=in_specs, out_specs=out_specs, check_vma=False)
```

```python
import functools

import jax
import jax.numpy as jnp
from jax import lax
from jax.experimental import pallas as pl
from jax.experimental.pallas import tpu as pltpu
from jax.sharding import PartitionSpec as P

K = 64
SWEEPS = 4
HALF = K // 2
TURNS = 8
STEPS = 4
LANES = 128
PINNED = 1e30
VMEM_BYTES = 16 * 1024 * 1024


def vmem():
    return pl.BlockSpec(memory_space=pltpu.VMEM)


def smem():
    return pl.BlockSpec(memory_space=pltpu.SMEM)


def hbm():
    return pl.BlockSpec(memory_space=pltpu.HBM)


def anywhere():
    return pl.BlockSpec(memory_space=pl.ANY)


def params():
    return pltpu.CompilerParams(vmem_limit_bytes=VMEM_BYTES)


def cost(flops, nbytes):
    return pl.CostEstimate(flops=flops, bytes_accessed=nbytes, transcendentals=0)


def shape_of(*shape):
    return jax.ShapeDtypeStruct(shape, jnp.float32)


def column_parity(rows, columns):
    return lax.broadcasted_iota(jnp.int32, (rows, columns), 1) % 2


def merge_rows(rows, keep):
    mask = column_parity(1, rows[0].shape[1]) == keep
    return jnp.concatenate([jnp.where(mask, rows[z], rows[z + 1]) for z in range(0, len(rows), 2)], axis=0)


def sends(ref, colour, core, odd, ze_ref, zi_ref, xe_ref, xo_ref):
    planes, rows, _ = ref.shape
    for j in range(0, rows, 8):
        at = pl.ds(j, 8)
        low, high = ref[0, at, :], ref[planes - 1, at, :]
        ze_ref[at, :] = jnp.where(core == 0, low, high)
        zi_ref[at, :] = jnp.where(core == 0, high, low)
    above = merge_rows([ref[z, pl.ds(rows - 1, 1), :] for z in range(planes)], 1 - colour)
    below = merge_rows([ref[z, pl.ds(0, 1), :] for z in range(planes)], colour)
    xe_ref[...] = jnp.where(odd == 0, above, below)
    xo_ref[...] = jnp.where(odd == 0, below, above)


def pack_kernel(where, pot_hbm, reg_hbm, chg_hbm, lev_ref, f0_ref, f1_ref, c0_ref, c1_ref, ze_ref, zi_ref, xe_ref,
                xo_ref, pot_ref, reg_ref, chg_ref, field, charge, sems):
    planes, rows, columns = f0_ref.shape
    tiles = rows // 8
    table = jnp.broadcast_to(lev_ref[...], (8, LANES))
    copies = [
        [
            pltpu.make_async_copy(source.at[z], target.at[z], sems.at[z, i])
            for i, (source, target) in enumerate(((reg_hbm, reg_ref), (pot_hbm, pot_ref), (chg_hbm, chg_ref)))
        ]
        for z in range(planes)
    ]
    for plane in copies:
        for copy in plane:
            copy.start()
    for z in range(planes):
        even = column_parity(8, LANES) == z % 2
        for copy in copies[z]:
            copy.wait()
        for c in range(columns // LANES):
            at = pl.ds(LANES * c, LANES)
            slot = z % 2 * (columns // LANES) + c
            for j in range(0, 2 * rows, 8):
                to = pl.ds(j, 8)
                region = reg_ref[z, to, at]
                pinned = jnp.take_along_axis(table, region, axis=1)
                free = region == 0
                field[slot, to, :] = jnp.where(free, pot_ref[z, to, at], pinned)
                charge[slot, to, :] = jnp.where(free, chg_ref[z, to, at], PINNED)
            for source, out0, out1 in ((field, f0_ref, f1_ref), (charge, c0_ref, c1_ref)):
                for j in range(tiles):
                    a = source[slot, pl.ds(2 * j, 8, stride=2 * tiles), :]
                    b = source[slot, pl.ds(2 * j + 1, 8, stride=2 * tiles), :]
                    out0[z, pl.ds(8 * j, 8), at] = jnp.where(even, a, b)
                    out1[z, pl.ds(8 * j, 8), at] = jnp.where(even, b, a)
    sends(f1_ref, 1, where[0], where[1], ze_ref, zi_ref, xe_ref, xo_ref)


def send_shapes(planes, rows, columns):
    return [shape_of(rows, columns)] * 2 + [shape_of(planes // 2, columns)] * 2


def pack(where, potential, regions, charge, levels):
    planes, rows, columns = potential.shape
    table = jnp.pad(levels, (0, LANES - levels.shape[0]))[None, :]
    half = shape_of(planes, rows // 2, columns)
    whole = (planes, rows, columns)
    stage = pltpu.VMEM((2 * columns // LANES, rows, LANES), jnp.float32)
    return pl.pallas_call(
        pack_kernel,
        in_specs=[smem(), hbm(), hbm(), hbm(), vmem()],
        out_specs=[vmem()] * 8,
        out_shape=[half] * 4 + send_shapes(*half.shape),
        scratch_shapes=[
            pltpu.VMEM(whole, jnp.float32),
            pltpu.VMEM(whole, jnp.int32),
            pltpu.VMEM(whole, jnp.float32),
            stage,
            stage,
            pltpu.SemaphoreType.DMA((planes, 3)),
        ],
        compiler_params=params(),
        name="pack",
    )(where, potential, regions, charge, table)


def relax(where, own_ref, other_ref, charge_ref, ze_ref, zi_ref, xe_ref, xo_ref, colour, put):
    core, odd, far_live, below_live, above_live = (where[i] for i in range(5))
    planes, rows, columns = own_ref.shape
    tiles = rows // 8
    row = lax.broadcasted_iota(jnp.int32, (8, columns), 0)
    lane = lax.broadcasted_iota(jnp.int32, (8, LANES), 1)
    parity = column_parity(8, columns)
    xe, xo = xe_ref[...], xo_ref[...]
    below = jnp.where(below_live == 1, jnp.where(odd == 0, xo, xe), 0.0)
    above = jnp.where(above_live == 1, jnp.where(odd == 0, xe, xo), 0.0)

    for z in range(planes):
        first_row = parity == (z + colour) % 2
        for j in range(tiles):
            at = pl.ds(8 * j, 8)
            tile = lambda t: other_ref[z, pl.ds(8 * t, 8), :]
            mid = tile(j)
            if z in (0, planes - 1):
                far = jnp.where(far_live == 1, ze_ref[at, :], 0.0)
                near = zi_ref[at, :]
            z_low = other_ref[z - 1, at, :] if z else jnp.where(core == 0, far, near)
            z_high = other_ref[z + 1, at, :] if z < planes - 1 else jnp.where(core == 0, near, far)
            if j:
                x_low = tile(j - 1)
            else:
                x_low = jnp.where(row == 0, below[z // 2 : z // 2 + 1], pltpu.roll(tile(tiles - 1), 1, 0))
            if j < tiles - 1:
                x_high = tile(j + 1)
            else:
                x_high = jnp.where(row == 7, above[z // 2 : z // 2 + 1], pltpu.roll(tile(0), 7, 0))
            y_low, y_high = pltpu.roll(mid, 1, 1), pltpu.roll(mid, columns - 1, 1)
            y_low = jnp.concatenate([jnp.where(lane == 0, 0.0, y_low[:, :LANES]), y_low[:, LANES:]], axis=1)
            y_high = jnp.concatenate(
                [y_high[:, :-LANES], jnp.where(lane == LANES - 1, 0.0, y_high[:, -LANES:])], axis=1
            )
            charge = charge_ref[z, at, :]
            beside = z_low + z_high + mid + jnp.where(first_row, x_low, x_high) + y_low + y_high
            own = own_ref[z, at, :]
            put(z, j, jnp.where(charge < PINNED, 0.25 * (beside + charge) - 0.5 * own, own))


def relax_kernel(colour, where, own_ref, other_ref, charge_ref, ze_ref, zi_ref, xe_ref, xo_ref, after,
                 out_ref, ze_out, zi_out, xe_out, xo_out):
    del after

    def put(z, j, value):
        out_ref[z, pl.ds(8 * j, 8), :] = value

    relax(where, own_ref, other_ref, charge_ref, ze_ref, zi_ref, xe_ref, xo_ref, colour, put)
    sends(out_ref, colour, where[0], where[1], ze_out, zi_out, xe_out, xo_out)


def half_sweep(where, own, other, charge, halos, colour, after):
    return pl.pallas_call(
        functools.partial(relax_kernel, colour),
        in_specs=[smem()] + [vmem()] * 7 + [anywhere()],
        out_specs=[vmem()] * 5,
        out_shape=[shape_of(*own.shape)] + send_shapes(*own.shape),
        compiler_params=params(),
        cost_estimate=cost(14 * own.size, 0),
        name="relax",
    )(where, own, other, charge, *halos, after)


def split(value):
    high = value.astype(jnp.bfloat16)
    return high, (value - high.astype(jnp.float32)).astype(jnp.bfloat16)


def angles_kernel(rows_total, tiles, columns, offset, start, after, left_ref, radial_ref, done_ref):
    del after
    done_ref[...] = jnp.zeros_like(done_ref)
    shape = (8, columns)
    column = lax.broadcasted_iota(jnp.int32, shape, 1)
    v = (column.astype(jnp.float32) + 0.5) * (2.0 / columns) - 1.0
    for j in range(tiles):
        packed = lax.broadcasted_iota(jnp.int32, shape, 0) * tiles + j
        row = start[0] + 2 * packed + (column + offset) % 2
        u = (row.astype(jnp.float32) + 0.5) * (2.0 / rows_total) - 1.0
        inverse = lax.rsqrt(u * u + v * v)
        c1, s1 = u * inverse, v * inverse
        c2, s2 = c1 * c1 - s1 * s1, 2.0 * (c1 * s1)
        c4, s4 = c2 * c2 - s2 * s2, 2.0 * (c2 * s2)
        u2, v2 = u * c1 - v * s1, u * s1 + v * c1
        u3, v3 = u2 * c1 - v2 * s1, u2 * s1 + v2 * c1
        u4, v4 = u2 * c2 - v2 * s2, u2 * s2 + v2 * c2
        for m, value in enumerate((u, u2, u3, u4, v, v2, v3, v4)):
            radial_ref[j, pl.ds(8 * m, 8), :] = value

        def put(index, value):
            high, low = split(value)
            left_ref[j, pl.ds(8 * index, 8), :] = high
            left_ref[j, pl.ds(8 * (2 * TURNS + index), 8), :] = low

        twice = 2.0 * c4
        c_old, s_old, c_now, s_now = jnp.ones_like(c4), jnp.zeros_like(c4), c4, s4
        put(0, c_old)
        put(TURNS, s_old)
        for a in range(1, TURNS):
            put(a, c_now)
            put(TURNS + a, s_now)
            c_old, s_old, c_now, s_now = c_now, s_now, twice * c_now - c_old, twice * s_now - s_old


def angles(start, after, rows_total, tiles, columns, offset):
    left = jax.ShapeDtypeStruct((tiles, 32 * TURNS, columns), jnp.bfloat16)
    return pl.pallas_call(
        functools.partial(angles_kernel, rows_total, tiles, columns, offset),
        in_specs=[smem(), anywhere()],
        out_specs=[vmem()] * 3,
        out_shape=[left, shape_of(tiles, 16 * STEPS, columns), shape_of(8, LANES)],
        compiler_params=params(),
        cost_estimate=cost(128 * tiles * 8 * columns, 0),
        name="angles",
    )(start, after)


def multipoles_of(colour, field_of, tables, out_ref, right):
    planes = out_ref.shape[0]
    pairs = planes // 2
    n, m = 16 * TURNS, 16 * STEPS * pairs
    tiles = tables[0][0].shape[0]
    for e in (0, 1):
        left_ref, radial_ref = tables[e]
        total = None
        for j in range(tiles):
            slot = (e * tiles + j) % right.shape[0]
            for k in range(pairs):
                f = field_of(2 * k + (e + colour) % 2, j)
                for b in range(2 * STEPS):
                    high, low = split(f * radial_ref[j, pl.ds(8 * b, 8), :])
                    index = 2 * STEPS * k + b
                    right[slot, pl.ds(8 * index, 8), :] = high
                    right[slot, pl.ds(m + 8 * index, 8), :] = low
            product = lax.dot_general(
                left_ref[j], right[slot], (((1,), (1,)), ((), ())), preferred_element_type=jnp.float32
            )
            total = product if total is None else total + product
        total = (total[:n, :m] + total[n:, :m]) + (total[:n, m:] + total[n:, m:])
        i = lax.broadcasted_iota(jnp.int32, total.shape, 0)
        k = lax.broadcasted_iota(jnp.int32, total.shape, 1)
        total = jnp.sum(jnp.where(i % 8 == k % 8, total, 0.0).reshape(2 * TURNS, 8, m), axis=1)
        for k in range(pairs):
            out_ref[2 * k + (e + colour) % 2] = total[:, 16 * STEPS * k : 16 * STEPS * (k + 1)]


def right_scratch(planes, columns):
    return pltpu.VMEM((2, 16 * STEPS * planes, columns), jnp.bfloat16)


def sums_shape(planes):
    return shape_of(planes, 2 * TURNS, 16 * STEPS)


def multipole_kernel(field_ref, left0, radial0, left1, radial1, out_ref, done_ref, right):
    done_ref[...] = jnp.zeros_like(done_ref)
    multipoles_of(0, lambda z, j: field_ref[z, pl.ds(8 * j, 8), :], ((left0, radial0), (left1, radial1)), out_ref,
                  right)


def multipole_sums(field, tables):
    planes, _, columns = field.shape
    return pl.pallas_call(
        multipole_kernel,
        in_specs=[vmem()] * 5,
        out_specs=[vmem()] * 2,
        out_shape=[sums_shape(planes), shape_of(8, LANES)],
        scratch_shapes=[right_scratch(planes, columns)],
        compiler_params=params(),
        cost_estimate=cost(100 * field.size, 0),
        name="multipole",
    )(field, *tables)


def last_kernel(where, own_ref, other_ref, charge_ref, ze_ref, zi_ref, xe_ref, xo_ref, left0, radial0, left1, radial1,
                after, field_hbm, out_ref, one, staged, right, sems):
    del after
    planes, rows, columns = own_ref.shape
    tiles = rows // 8
    copies = []

    def put(z, j, value):
        one[z, pl.ds(8 * j, 8), :] = value
        even = column_parity(8, columns) == z % 2
        zero = other_ref[z, pl.ds(8 * j, 8), :]
        low, high = jnp.where(even, zero, value), jnp.where(even, value, zero)
        for c in range(columns // LANES):
            at = slice(LANES * c, LANES * c + LANES)
            staged[z, c, pl.ds(2 * j, 8, stride=2 * tiles), :] = low[:, at]
            staged[z, c, pl.ds(2 * j + 1, 8, stride=2 * tiles), :] = high[:, at]
            if j == tiles - 1:
                copy = pltpu.make_async_copy(
                    staged.at[z, c], field_hbm.at[z, :, pl.ds(LANES * c, LANES)], sems.at[z, c]
                )
                copy.start()
                copies.append(copy)

    relax(where, own_ref, other_ref, charge_ref, ze_ref, zi_ref, xe_ref, xo_ref, 1, put)
    multipoles_of(1, lambda z, j: one[z, pl.ds(8 * j, 8), :], ((left0, radial0), (left1, radial1)), out_ref, right)
    for copy in copies:
        copy.wait()


def last_half_sweep(where, own, other, charge, halos, tables, after):
    planes, rows, columns = own.shape
    return pl.pallas_call(
        last_kernel,
        in_specs=[smem()] + [vmem()] * 11 + [anywhere()],
        out_specs=[hbm(), vmem()],
        out_shape=[shape_of(planes, 2 * rows, columns), sums_shape(planes)],
        scratch_shapes=[
            pltpu.VMEM(own.shape, jnp.float32),
            pltpu.VMEM((planes, columns // LANES, 2 * rows, LANES), jnp.float32),
            right_scratch(planes, columns),
            pltpu.SemaphoreType.DMA((planes, columns // LANES)),
        ],
        compiler_params=params(),
        cost_estimate=cost(100 * own.size, 0),
        name="relax_last",
    )(where, own, other, charge, *halos, *tables, after)


def swaps(pairs):
    return [(a, b) for a, b in pairs] + [(b, a) for a, b in pairs]


def odd_swaps(count):
    return swaps([(i, i + 1) for i in range(1, count - 1, 2)]) + [(0, 0), (count - 1, count - 1)]


def local(potential, regions, charge, levels):
    planes, row_count, columns = potential.shape
    gx, gz = lax.axis_index("gx"), lax.axis_index("gz")
    nx, nz = lax.axis_size("gx"), lax.axis_size("gz")
    rows_total = nx * row_count
    tiles = row_count // 16
    core = gz % 2
    where = jnp.stack(
        [core, gx % 2, jnp.where(core == 0, gz > 0, gz < nz - 1), gx > 0, gx < nx - 1, gx * row_count]
    ).astype(jnp.int32)
    start = where[5:]
    z_far, z_near = odd_swaps(nz), [(i, i ^ 1) for i in range(nz)]
    x_even, x_odd = [(i, i ^ 1) for i in range(nx)], odd_swaps(nx)

    def exchange(ze, zi, xe, xo):
        return (
            lax.ppermute(ze, "gz", z_far),
            lax.ppermute(zi, "gz", z_near),
            lax.ppermute(xe, "gx", x_even),
            lax.ppermute(xo, "gx", x_odd),
        )

    zero, one, charge0, charge1, *out = pack(where, potential, regions, charge, levels)
    after, tables = where, []
    for sweep in range(SWEEPS):
        halos = exchange(*out)
        zero, *out = half_sweep(where, zero, one, charge0, halos, 0, after)
        halos = exchange(*out)
        after = where
        if sweep < SWEEPS - 1:
            if sweep < 2:
                *table, after = angles(start, out[2], rows_total, tiles, columns, sweep)
                tables += table
            one, *out = half_sweep(where, one, zero, charge1, halos, 1, after)
            after = where
    sums0, after = multipole_sums(zero, tables)
    field, sums1 = last_half_sweep(where, one, zero, charge1, halos, tables, after)
    sums = (sums0 + sums1).reshape(planes, 2, TURNS, 2, STEPS, 8).sum(-1)
    cos_part = sums[:, 0, :, 0] - sums[:, 1, :, 1]
    sin_part = sums[:, 1, :, 0] + sums[:, 0, :, 1]
    part = jnp.concatenate([cos_part.reshape(planes, HALF), sin_part.reshape(planes, HALF)], axis=1)
    part = part * (1.0 / jnp.sqrt(jnp.float32(rows_total) * jnp.float32(columns)))
    share = K // nx
    part = jnp.transpose(part.reshape(planes, nx, share), (1, 0, 2))
    shares = lax.all_to_all(part, "gx", 0, 0, tiled=True)
    return field, jnp.sum(shares, axis=0)


def solution(mesh):
    in_specs = (P("gz", "gx", None), P("gz", "gx", None), P("gz", "gx", None), P())
    out_specs = (P("gz", "gx", None), P("gz", "gx"))
    return jax.shard_map(local, mesh=mesh, in_specs=in_specs, out_specs=out_specs, check_vma=False)
```

```python
import functools
import math

import jax
import jax.numpy as jnp
from jax import lax
from jax.experimental import pallas as pl
from jax.experimental.pallas import tpu as pltpu
from jax.sharding import PartitionSpec as P

K = 64
SWEEPS = 4
HALF = K // 2
TURNS = 8
STEPS = 4
LANES = 128
PINNED = 1e30
VMEM_BYTES = 16 * 1024 * 1024
PACK_VMEM_BYTES = 50 * 1024 * 1024


def vmem():
    return pl.BlockSpec(memory_space=pltpu.VMEM)


def smem():
    return pl.BlockSpec(memory_space=pltpu.SMEM)


def hbm():
    return pl.BlockSpec(memory_space=pltpu.HBM)


def anywhere():
    return pl.BlockSpec(memory_space=pl.ANY)


def params():
    return pltpu.CompilerParams(vmem_limit_bytes=VMEM_BYTES)


def cost(flops, nbytes):
    return pl.CostEstimate(flops=flops, bytes_accessed=nbytes, transcendentals=0)


def shape_of(*shape):
    return jax.ShapeDtypeStruct(shape, jnp.float32)


def column_parity(rows, columns):
    return lax.broadcasted_iota(jnp.int32, (rows, columns), 1) % 2


def chunks(columns):
    return [(c, pl.ds(LANES * c, LANES)) for c in range(columns // LANES)]


def sends(ref, colour, core, odd, ze_ref, zi_ref, xe_ref, xo_ref):
    planes, rows, columns = ref.shape
    count = columns // LANES
    parity = column_parity(8, LANES)

    def sides(low_ref, high_ref, above_ref, below_ref):
        for j in range(0, rows, 8):
            for _, at in chunks(columns):
                low_ref[pl.ds(j, 8), at] = ref[0, pl.ds(j, 8), at]
                high_ref[pl.ds(j, 8), at] = ref[planes - 1, pl.ds(j, 8), at]
        for k in range(planes // 2):
            for c, at in chunks(columns):
                line = pl.ds(k * count + c, 1)
                last = [ref[2 * k + i, pl.ds(rows - 8, 8), at] for i in (0, 1)]
                first = [ref[2 * k + i, pl.ds(0, 8), at] for i in (0, 1)]
                above_ref[line, :] = jnp.where(parity == 1 - colour, last[0], last[1])[7:8]
                below_ref[line, :] = jnp.where(parity == colour, first[0], first[1])[0:1]

    for c in (0, 1):
        for o in (0, 1):

            @pl.when((core == c) & (odd == o))
            def _():
                z_refs = (zi_ref, ze_ref) if c else (ze_ref, zi_ref)
                x_refs = (xo_ref, xe_ref) if o else (xe_ref, xo_ref)
                sides(*z_refs, *x_refs)


def pack_kernel(where, pot_hbm, reg_hbm, chg_hbm, lev_ref, f0_ref, f1_ref, c0_ref, c1_ref, ze_ref, zi_ref, xe_ref,
                xo_ref, pot_ref, reg_ref, chg_ref, field, charge, sems):
    planes, rows, columns = f0_ref.shape
    tiles = rows // 8
    table = jnp.broadcast_to(lev_ref[...], (8, LANES))
    copies = [
        [
            pltpu.make_async_copy(source.at[z], target.at[z], sems.at[z, i])
            for i, (source, target) in enumerate(((reg_hbm, reg_ref), (pot_hbm, pot_ref), (chg_hbm, chg_ref)))
        ]
        for z in range(planes)
    ]
    for plane in copies:
        for copy in plane:
            copy.start()
    for z in range(planes):
        even = column_parity(8, LANES) == z % 2
        for copy in copies[z]:
            copy.wait()
        for c in range(columns // LANES):
            at = pl.ds(LANES * c, LANES)
            slot = z % 2 * (columns // LANES) + c
            for j in range(0, 2 * rows, 8):
                to = pl.ds(j, 8)
                region = reg_ref[z, to, at]
                pinned = jnp.take_along_axis(table, region, axis=1)
                free = region == 0
                field[slot, to, :] = jnp.where(free, pot_ref[z, to, at], pinned)
                charge[slot, to, :] = jnp.where(free, chg_ref[z, to, at], PINNED)
            for source, out0, out1 in ((field, f0_ref, f1_ref), (charge, c0_ref, c1_ref)):
                for j in range(tiles):
                    a = source[slot, pl.ds(2 * j, 8, stride=2 * tiles), :]
                    b = source[slot, pl.ds(2 * j + 1, 8, stride=2 * tiles), :]
                    out0[z, pl.ds(8 * j, 8), at] = jnp.where(even, a, b)
                    out1[z, pl.ds(8 * j, 8), at] = jnp.where(even, b, a)
    sends(f1_ref, 1, where[0], where[1], ze_ref, zi_ref, xe_ref, xo_ref)


def send_shapes(planes, rows, columns):
    return [shape_of(rows, columns)] * 2 + [shape_of(planes // 2 * columns // LANES, LANES)] * 2


def pack(where, potential, regions, charge, levels):
    planes, rows, columns = potential.shape
    table = jnp.pad(levels, (0, LANES - levels.shape[0]))[None, :]
    half = shape_of(planes, rows // 2, columns)
    whole = (planes, rows, columns)
    stage = pltpu.VMEM((2 * columns // LANES, rows, LANES), jnp.float32)
    return pl.pallas_call(
        pack_kernel,
        in_specs=[smem(), hbm(), hbm(), hbm(), vmem()],
        out_specs=[vmem()] * 8,
        out_shape=[half] * 4 + send_shapes(*half.shape),
        scratch_shapes=[
            pltpu.VMEM(whole, jnp.float32),
            pltpu.VMEM(whole, jnp.int32),
            pltpu.VMEM(whole, jnp.float32),
            stage,
            stage,
            pltpu.SemaphoreType.DMA((planes, 3)),
        ],
        compiler_params=pltpu.CompilerParams(vmem_limit_bytes=PACK_VMEM_BYTES),
        name="pack",
    )(where, potential, regions, charge, table)


def relax(where, own_ref, other_ref, charge_ref, ze_ref, zi_ref, xe_ref, xo_ref, below, above, colour, put):
    core, odd, far_live, below_live, above_live = (where[i] for i in range(5))
    planes, rows, columns = own_ref.shape
    tiles, count = rows // 8, columns // LANES
    row = lax.broadcasted_iota(jnp.int32, (8, LANES), 0)
    lane = lax.broadcasted_iota(jnp.int32, (8, LANES), 1)
    parity = column_parity(8, LANES)
    xe, xo = xe_ref[...], xo_ref[...]
    below[...] = jnp.where(below_live == 1, jnp.where(odd == 0, xo, xe), 0.0)
    above[...] = jnp.where(above_live == 1, jnp.where(odd == 0, xe, xo), 0.0)

    for z in range(planes):
        first_row = parity == (z + colour) % 2
        for j in range(tiles):
            rows_at = pl.ds(8 * j, 8)
            for c, at in chunks(columns):
                tile = lambda t, at=at: other_ref[z, pl.ds(8 * t, 8), at]
                mid = tile(j)
                if z in (0, planes - 1):
                    far = jnp.where(far_live == 1, ze_ref[rows_at, at], 0.0)
                    near = zi_ref[rows_at, at]
                z_low = other_ref[z - 1, rows_at, at] if z else jnp.where(core == 0, far, near)
                z_high = other_ref[z + 1, rows_at, at] if z < planes - 1 else jnp.where(core == 0, near, far)
                line = pl.ds(z // 2 * count + c, 1)
                if j:
                    x_low = tile(j - 1)
                else:
                    x_low = jnp.where(row == 0, below[line, :], pltpu.roll(tile(tiles - 1), 1, 0))
                if j < tiles - 1:
                    x_high = tile(j + 1)
                else:
                    x_high = jnp.where(row == 7, above[line, :], pltpu.roll(tile(0), 7, 0))
                left = other_ref[z, rows_at, pl.ds(LANES * (c - 1), LANES)] if c else 0.0
                right = other_ref[z, rows_at, pl.ds(LANES * (c + 1), LANES)] if c < count - 1 else 0.0
                y_low = pltpu.roll(jnp.where(lane == LANES - 1, left, mid), 1, 1)
                y_high = pltpu.roll(jnp.where(lane == 0, right, mid), LANES - 1, 1)
                charge = charge_ref[z, rows_at, at]
                beside = z_low + z_high + mid + jnp.where(first_row, x_low, x_high) + y_low + y_high
                own = own_ref[z, rows_at, at]
                put(z, j, c, jnp.where(charge < PINNED, 0.25 * (beside + charge) - 0.5 * own, own))


def line_scratch(planes, columns):
    return [pltpu.VMEM((planes // 2 * columns // LANES, LANES), jnp.float32)] * 2


def relax_kernel(colour, where, own_ref, other_ref, charge_ref, ze_ref, zi_ref, xe_ref, xo_ref, after,
                 out_ref, ze_out, zi_out, xe_out, xo_out, below, above):
    del after

    def put(z, j, c, value):
        out_ref[z, pl.ds(8 * j, 8), pl.ds(LANES * c, LANES)] = value

    relax(where, own_ref, other_ref, charge_ref, ze_ref, zi_ref, xe_ref, xo_ref, below, above, colour, put)
    sends(out_ref, colour, where[0], where[1], ze_out, zi_out, xe_out, xo_out)


def half_sweep(where, own, other, charge, halos, colour, after):
    return pl.pallas_call(
        functools.partial(relax_kernel, colour),
        in_specs=[smem()] + [vmem()] * 7 + [anywhere()],
        out_specs=[vmem()] * 5,
        out_shape=[shape_of(*own.shape)] + send_shapes(*own.shape),
        scratch_shapes=line_scratch(own.shape[0], own.shape[2]),
        compiler_params=params(),
        cost_estimate=cost(14 * own.size, 0),
        name="relax",
    )(where, own, other, charge, *halos, after)


def split(value):
    high = value.astype(jnp.bfloat16)
    return high, (value - high.astype(jnp.float32)).astype(jnp.bfloat16)


def angles_kernel(rows_total, tiles, columns, offset, start, after, left_ref, radial_ref, done_ref):
    del after
    done_ref[...] = jnp.zeros_like(done_ref)
    shape = (8, columns)
    column = lax.broadcasted_iota(jnp.int32, shape, 1)
    v = (column.astype(jnp.float32) + 0.5) * (2.0 / columns) - 1.0
    for j in range(tiles):
        packed = lax.broadcasted_iota(jnp.int32, shape, 0) * tiles + j
        row = start[0] + 2 * packed + (column + offset) % 2
        u = (row.astype(jnp.float32) + 0.5) * (2.0 / rows_total) - 1.0
        inverse = lax.rsqrt(u * u + v * v)
        c1, s1 = u * inverse, v * inverse
        c2, s2 = c1 * c1 - s1 * s1, 2.0 * (c1 * s1)
        c4, s4 = c2 * c2 - s2 * s2, 2.0 * (c2 * s2)
        u2, v2 = u * c1 - v * s1, u * s1 + v * c1
        u3, v3 = u2 * c1 - v2 * s1, u2 * s1 + v2 * c1
        u4, v4 = u2 * c2 - v2 * s2, u2 * s2 + v2 * c2
        for m, value in enumerate((u, u2, u3, u4, v, v2, v3, v4)):
            radial_ref[j, pl.ds(8 * m, 8), :] = value

        def put(index, pair):
            high, low = split(jnp.concatenate(pair, axis=0))
            left_ref[j, pl.ds(8 * index, 16), :] = high
            left_ref[j, pl.ds(8 * (2 * TURNS + index), 16), :] = low

        twice = 2.0 * c4
        cosines, sines = [jnp.ones_like(c4), c4], [jnp.zeros_like(c4), s4]
        for a in range(0, TURNS, 2):
            put(a, cosines)
            put(TURNS + a, sines)
            for terms in (cosines, sines):
                terms[0] = twice * terms[1] - terms[0]
                terms[1] = twice * terms[0] - terms[1]


def angles(start, after, rows_total, tiles, columns, offset):
    left = jax.ShapeDtypeStruct((tiles, 32 * TURNS, columns), jnp.bfloat16)
    return pl.pallas_call(
        functools.partial(angles_kernel, rows_total, tiles, columns, offset),
        in_specs=[smem(), anywhere()],
        out_specs=[vmem()] * 3,
        out_shape=[left, shape_of(tiles, 16 * STEPS, columns), shape_of(8, LANES)],
        compiler_params=params(),
        cost_estimate=cost(128 * tiles * 8 * columns, 0),
        name="angles",
    )(start, after)


def multipoles_of(colour, field_of, tables, planes, right):
    out = jnp.zeros((TURNS, 2 * STEPS * planes), jnp.float32)
    pairs = planes // 2
    n, m = 16 * TURNS, 16 * STEPS * pairs
    tiles = tables[0][0].shape[0]
    for e in (0, 1):
        left_ref, radial_ref = tables[e]
        total = None
        for j in range(tiles):
            slot = (e * tiles + j) % right.shape[0]
            for k in range(pairs):
                f = field_of(2 * k + (e + colour) % 2, j)
                twice = jnp.concatenate([f, f], axis=0)
                for b in range(0, 2 * STEPS, 2):
                    high, low = split(twice * radial_ref[j, pl.ds(8 * b, 16), :])
                    index = 2 * STEPS * k + b
                    right[slot, pl.ds(8 * index, 16), :] = high
                    right[slot, pl.ds(m + 8 * index, 16), :] = low
            product = lax.dot_general(
                left_ref[j], right[slot], (((1,), (1,)), ((), ())), preferred_element_type=jnp.float32
            )
            total = product if total is None else total + product
        total = (total[:n, :m] + total[n:, :m]) + (total[:n, m:] + total[n:, m:])
        i = lax.broadcasted_iota(jnp.int32, total.shape, 0)
        k = lax.broadcasted_iota(jnp.int32, total.shape, 1)
        total = jnp.sum(jnp.where(i % 8 == k % 8, total, 0.0).reshape(2 * TURNS, 8, m), axis=1)
        exact = functools.partial(
            jnp.dot, preferred_element_type=jnp.float32, precision=lax.Precision.HIGHEST
        )
        width = 2 * STEPS * planes
        term = lax.broadcasted_iota(jnp.int32, (m, width), 0) // 8
        column = lax.broadcasted_iota(jnp.int32, (m, width), 1)
        pair, sine, b = term // (2 * STEPS), term // STEPS % 2, term % STEPS
        base = (2 * pair + (e + colour) % 2) * 2 * STEPS + b
        same = (column == base + sine * STEPS).astype(jnp.float32)
        cross = jnp.where(column == base + (1 - sine) * STEPS, jnp.where(sine == 0, 1.0, -1.0), 0.0)
        out = out + exact(total[:TURNS], same) + exact(total[TURNS:], cross)
    return out


def right_scratch(planes, columns):
    return pltpu.VMEM((2, 16 * STEPS * planes, columns), jnp.bfloat16)


def sums_shape(planes):
    return shape_of(TURNS, 2 * STEPS * planes)


def multipole_kernel(field_ref, left0, radial0, left1, radial1, out_ref, done_ref, right):
    done_ref[...] = jnp.zeros_like(done_ref)
    out_ref[...] = multipoles_of(
        0,
        lambda z, j: field_ref[z, pl.ds(8 * j, 8), :],
        ((left0, radial0), (left1, radial1)),
        field_ref.shape[0],
        right,
    )


def multipole_sums(field, tables):
    planes, _, columns = field.shape
    return pl.pallas_call(
        multipole_kernel,
        in_specs=[vmem()] * 5,
        out_specs=[vmem()] * 2,
        out_shape=[sums_shape(planes), shape_of(8, LANES)],
        scratch_shapes=[right_scratch(planes, columns)],
        compiler_params=params(),
        cost_estimate=cost(100 * field.size, 0),
        name="multipole",
    )(field, *tables)


def last_kernel(scale, where, own_ref, other_ref, charge_ref, ze_ref, zi_ref, xe_ref, xo_ref, left0, radial0, left1,
                radial1, sums_ref, after, field_hbm, out_ref, one, staged, right, below, above, sems):
    del after
    planes, rows, columns = own_ref.shape
    tiles = rows // 8
    copies = []

    def put(z, j, c, value):
        at = pl.ds(LANES * c, LANES)
        one[z, pl.ds(8 * j, 8), at] = value
        even = column_parity(8, LANES) == z % 2
        zero = other_ref[z, pl.ds(8 * j, 8), at]
        staged[z, c, pl.ds(2 * j, 8, stride=2 * tiles), :] = jnp.where(even, zero, value)
        staged[z, c, pl.ds(2 * j + 1, 8, stride=2 * tiles), :] = jnp.where(even, value, zero)
        if j == tiles - 1:
            copy = pltpu.make_async_copy(staged.at[z, c], field_hbm.at[z, :, at], sems.at[z, c])
            copy.start()
            copies.append(copy)

    relax(where, own_ref, other_ref, charge_ref, ze_ref, zi_ref, xe_ref, xo_ref, below, above, 1, put)
    sums = multipoles_of(
        1, lambda z, j: one[z, pl.ds(8 * j, 8), :], ((left0, radial0), (left1, radial1)), planes, right
    )
    out_ref[...] = (sums + sums_ref[...]) * scale
    for copy in copies:
        copy.wait()


def last_half_sweep(where, own, other, charge, halos, tables, sums, after, scale):
    planes, rows, columns = own.shape
    return pl.pallas_call(
        functools.partial(last_kernel, scale),
        in_specs=[smem()] + [vmem()] * 12 + [anywhere()],
        out_specs=[hbm(), vmem()],
        out_shape=[shape_of(planes, 2 * rows, columns), sums_shape(planes)],
        scratch_shapes=[
            pltpu.VMEM(own.shape, jnp.float32),
            pltpu.VMEM((planes, columns // LANES, 2 * rows, LANES), jnp.float32),
            right_scratch(planes, columns),
            *line_scratch(planes, columns),
            pltpu.SemaphoreType.DMA((planes, columns // LANES)),
        ],
        compiler_params=params(),
        cost_estimate=cost(100 * own.size, 0),
        name="relax_last",
    )(where, own, other, charge, *halos, *tables, sums, after)


def swaps(pairs):
    return [(a, b) for a, b in pairs] + [(b, a) for a, b in pairs]


def far_pairs(nx, nz):
    pairs = [(x * nz + z, x * nz + z + 1) for x in range(nx) for z in range(1, nz - 1, 2)]
    return swaps(pairs + [(x * nz + z, (x + 1) * nz + z) for x in range(0, nx, 2) for z in (0, nz - 1)])


def odd_pairs(nx, nz):
    pairs = [(x * nz + z, (x + 1) * nz + z) for x in range(1, nx - 1, 2) for z in range(nz)]
    return swaps(pairs + [(x * nz + z, x * nz + z + 1) for x in (0, nx - 1) for z in range(0, nz, 2)])


def local(potential, regions, charge, levels):
    planes, row_count, columns = potential.shape
    gx, gz = lax.axis_index("gx"), lax.axis_index("gz")
    nx, nz = lax.axis_size("gx"), lax.axis_size("gz")
    rows_total = nx * row_count
    tiles = row_count // 16
    core = gz % 2
    where = jnp.stack(
        [core, gx % 2, jnp.where(core == 0, gz > 0, gz < nz - 1), gx > 0, gx < nx - 1, gx * row_count]
    ).astype(jnp.int32)
    start = where[5:]
    z_near, x_even = [(i, i ^ 1) for i in range(nz)], [(i, i ^ 1) for i in range(nx)]
    z_far, x_odd = far_pairs(nx, nz), odd_pairs(nx, nz)

    def exchange(ze, zi, xe, xo):
        ze = lax.ppermute(ze, ("gx", "gz"), z_far)
        xo = lax.ppermute(xo, ("gx", "gz"), x_odd)
        xe = lax.ppermute(xe, "gx", x_even)
        zi = lax.ppermute(zi, "gz", z_near)
        return ze, zi, xe, xo

    zero, one, charge0, charge1, *out = pack(where, potential, regions, charge, levels)
    after, tables = where, []
    for sweep in range(SWEEPS):
        halos = exchange(*out)
        zero, *out = half_sweep(where, zero, one, charge0, halos, 0, after)
        halos = exchange(*out)
        after = where
        if sweep < SWEEPS - 1:
            if sweep < 2:
                *table, after = angles(start, out[2], rows_total, tiles, columns, sweep)
                tables += table
            one, *out = half_sweep(where, one, zero, charge1, halos, 1, after)
            after = where
    sums, after = multipole_sums(zero, tables)
    scale = 1.0 / math.sqrt(rows_total * columns)
    field, sums = last_half_sweep(where, one, zero, charge1, halos, tables, sums, after, scale)
    share = K // nx
    parts = jnp.transpose(sums.reshape(TURNS, planes, 2, STEPS), (1, 2, 0, 3)).reshape(planes, nx, share)
    parts = jnp.transpose(parts, (1, 0, 2)).reshape(nx, planes * share)
    shares = lax.all_to_all(parts, "gx", 0, 0, tiled=True)
    return field, jnp.sum(shares, axis=0).reshape(planes, share)


def solution(mesh):
    in_specs = (P("gz", "gx", None), P("gz", "gx", None), P("gz", "gx", None), P())
    out_specs = (P("gz", "gx", None), P("gz", "gx"))
    return jax.shard_map(local, mesh=mesh, in_specs=in_specs, out_specs=out_specs, check_vma=False)
```

```python
import functools
import math

import jax
import jax.numpy as jnp
from jax import lax
from jax.experimental import pallas as pl
from jax.experimental.pallas import tpu as pltpu
from jax.sharding import PartitionSpec as P

K = 64
SWEEPS = 4
HALF = K // 2
TURNS = 8
STEPS = 4
LANES = 128
PARTS = 1
PITCH = 9
PINNED = 1e30
VMEM_BYTES = 16 * 1024 * 1024
PACK_VMEM_BYTES = 50 * 1024 * 1024


def vmem():
    return pl.BlockSpec(memory_space=pltpu.VMEM)


def smem():
    return pl.BlockSpec(memory_space=pltpu.SMEM)


def hbm():
    return pl.BlockSpec(memory_space=pltpu.HBM)


def anywhere():
    return pl.BlockSpec(memory_space=pl.ANY)


def params():
    return pltpu.CompilerParams(vmem_limit_bytes=VMEM_BYTES)


def cost(flops, nbytes):
    return pl.CostEstimate(flops=flops, bytes_accessed=nbytes, transcendentals=0)


def shape_of(*shape):
    return jax.ShapeDtypeStruct(shape, jnp.float32)


def column_parity(rows, columns):
    return lax.broadcasted_iota(jnp.int32, (rows, columns), 1) % 2


def chunks(columns):
    return [(c, pl.ds(LANES * c, LANES)) for c in range(columns // LANES)]


def position():
    gx, gz = lax.axis_index("gx"), lax.axis_index("gz")
    nx, nz = lax.axis_size("gx"), lax.axis_size("gz")
    core = gz % 2
    far = jnp.where(core == 0, gz > 0, gz < nz - 1)
    return core, gx % 2, far, gx > 0, gx < nx - 1


def sends(ref, colour, core, odd, ze_ref, xo_ref, xe_ref, zi_ref):
    planes, rows, columns = ref.shape
    count = columns // LANES
    parity = column_parity(8, LANES)

    def sides(low_ref, high_ref, above_ref, below_ref):
        for j in range(0, rows, 8):
            for _, at in chunks(columns):
                low_ref[pl.ds(j, 8), at] = ref[0, pl.ds(j, 8), at]
                high_ref[pl.ds(j, 8), at] = ref[planes - 1, pl.ds(j, 8), at]
        for k in range(planes // 2):
            for c, at in chunks(columns):
                line = pl.ds(k * count + c, 1)
                last = [ref[2 * k + i, pl.ds(rows - 8, 8), at] for i in (0, 1)]
                first = [ref[2 * k + i, pl.ds(0, 8), at] for i in (0, 1)]
                above_ref[line, :] = jnp.where(parity == 1 - colour, last[0], last[1])[7:8]
                below_ref[line, :] = jnp.where(parity == colour, first[0], first[1])[0:1]

    for c in (0, 1):
        for o in (0, 1):

            @pl.when((core == c) & (odd == o))
            def _():
                z_refs = (zi_ref, ze_ref) if c else (ze_ref, zi_ref)
                x_refs = (xo_ref, xe_ref) if o else (xe_ref, xo_ref)
                sides(*z_refs, *x_refs)


def spread_rows(source, tiles, even):
    for j in range(tiles):
        a = source[pl.ds(2 * j, 8, stride=2 * tiles), :]
        b = source[pl.ds(2 * j + 1, 8, stride=2 * tiles), :]
        yield pl.ds(8 * j, 8), jnp.where(even, a, b), jnp.where(even, b, a)


def pack_kernel(pot_hbm, reg_hbm, lev_hbm, f0_ref, f1_ref, m0_ref, m1_ref, ze_ref, xo_ref, xe_ref, zi_ref, lev_ref,
                pot_ref, reg_ref, field, mark, lev_sem, sems):
    planes, rows, columns = f0_ref.shape
    lev_copy = pltpu.make_async_copy(lev_hbm, lev_ref, lev_sem)
    lev_copy.start()
    copies = [
        [
            pltpu.make_async_copy(source.at[z], target.at[z], sems.at[z, i])
            for i, (source, target) in enumerate(((reg_hbm, reg_ref), (pot_hbm, pot_ref)))
        ]
        for z in range(planes)
    ]
    for plane in copies:
        for copy in plane:
            copy.start()
    lev_copy.wait()
    lane = lax.broadcasted_iota(jnp.int32, (8, LANES), 1)
    table = jnp.zeros((8, LANES), jnp.float32)
    for region in range(1, lev_ref.shape[0]):
        table = jnp.where(lane == region, lev_ref[region], table)
    for z in range(planes):
        even = column_parity(8, LANES) == z % 2
        for copy in copies[z]:
            copy.wait()
        for c, at in chunks(columns):
            slot = z % 2 * (columns // LANES) + c
            for j in range(0, 2 * rows, 8):
                to = pl.ds(j, 8)
                region = reg_ref[z, to, at]
                pinned = jnp.take_along_axis(table, region, axis=1)
                free = region == 0
                field[slot, to, :] = jnp.where(free, pot_ref[z, to, at], pinned)
                mark[slot, to, :] = jnp.where(free, 0.0, PINNED)
            for source, out0, out1 in ((field, f0_ref, f1_ref), (mark, m0_ref, m1_ref)):
                for to, a, b in spread_rows(source.at[slot], rows // 8, even):
                    out0[z, to, at] = a
                    out1[z, to, at] = b
    sends(f1_ref, 1, *position()[:2], ze_ref, xo_ref, xe_ref, zi_ref)


def send_shapes(planes, rows, columns):
    side, line = shape_of(rows, columns), shape_of(planes // 2 * columns // LANES, LANES)
    return [side, line, line, side]


def pack(potential, regions, levels):
    planes, rows, columns = potential.shape
    half = shape_of(planes, rows // 2, columns)
    whole = (planes, rows, columns)
    stage = pltpu.VMEM((2 * columns // LANES, rows, LANES), jnp.float32)
    return pl.pallas_call(
        pack_kernel,
        in_specs=[hbm()] * 3,
        out_specs=[vmem()] * 8,
        out_shape=[half] * 4 + send_shapes(*half.shape),
        scratch_shapes=[
            pltpu.SMEM(levels.shape, jnp.float32),
            pltpu.VMEM(whole, jnp.float32),
            pltpu.VMEM(whole, jnp.int32),
            stage,
            stage,
            pltpu.SemaphoreType.DMA,
            pltpu.SemaphoreType.DMA((planes, 2)),
        ],
        compiler_params=pltpu.CompilerParams(vmem_limit_bytes=PACK_VMEM_BYTES),
        cost_estimate=cost(20 * potential.size, 8 * potential.size),
        name="pack",
    )(potential, regions, levels)


def charge_kernel(chg_hbm, m0_ref, m1_ref, after, c0_ref, c1_ref, done_ref, chg_ref, stage, sems):
    del after
    done_ref[...] = jnp.zeros_like(done_ref)
    planes, rows, columns = m0_ref.shape
    copies = [pltpu.make_async_copy(chg_hbm.at[z], chg_ref.at[z], sems.at[z]) for z in range(planes)]
    for copy in copies:
        copy.start()
    for z in range(planes):
        even = column_parity(8, LANES) == z % 2
        copies[z].wait()
        for c, at in chunks(columns):
            slot = z % 2 * (columns // LANES) + c
            for j in range(0, 2 * rows, 8):
                stage[slot, pl.ds(j, 8), :] = chg_ref[z, pl.ds(j, 8), at]
            for to, a, b in spread_rows(stage.at[slot], rows // 8, even):
                c0_ref[z, to, at] = m0_ref[z, to, at] + a
                c1_ref[z, to, at] = m1_ref[z, to, at] + b


def pack_charge(charge, marks, after):
    planes, rows, columns = charge.shape
    half = shape_of(planes, rows // 2, columns)
    return pl.pallas_call(
        charge_kernel,
        in_specs=[hbm(), vmem(), vmem(), anywhere()],
        out_specs=[vmem()] * 3,
        out_shape=[half, half, shape_of(8, LANES)],
        scratch_shapes=[
            pltpu.VMEM(charge.shape, jnp.float32),
            pltpu.VMEM((2 * columns // LANES, rows, LANES), jnp.float32),
            pltpu.SemaphoreType.DMA((planes,)),
        ],
        compiler_params=pltpu.CompilerParams(vmem_limit_bytes=PACK_VMEM_BYTES),
        cost_estimate=cost(20 * charge.size, 4 * charge.size),
        name="charge",
    )(charge, *marks, after)


def relax(own_ref, other_ref, charge_ref, ze_ref, xo_ref, xe_ref, zi_ref, below, above, colour, put):
    core, odd, far_live, below_live, above_live = position()
    planes, rows, columns = own_ref.shape
    tiles, count = rows // 8, columns // LANES
    row = lax.broadcasted_iota(jnp.int32, (8, LANES), 0)
    lane = lax.broadcasted_iota(jnp.int32, (8, LANES), 1)
    parity = column_parity(8, LANES)
    xe, xo = xe_ref[...], xo_ref[...]
    below[...] = jnp.where(below_live, jnp.where(odd == 0, xo, xe), 0.0)
    above[...] = jnp.where(above_live, jnp.where(odd == 0, xe, xo), 0.0)

    for z in range(planes):
        first_row = parity == (z + colour) % 2
        for j in range(tiles):
            rows_at = pl.ds(8 * j, 8)
            for c, at in chunks(columns):
                tile = lambda t, at=at: other_ref[z, pl.ds(8 * t, 8), at]
                mid = tile(j)
                if z in (0, planes - 1):
                    far = jnp.where(far_live, ze_ref[rows_at, at], 0.0)
                    near = zi_ref[rows_at, at]
                z_low = other_ref[z - 1, rows_at, at] if z else jnp.where(core == 0, far, near)
                z_high = other_ref[z + 1, rows_at, at] if z < planes - 1 else jnp.where(core == 0, near, far)
                line = pl.ds(z // 2 * count + c, 1)
                if j:
                    x_low = tile(j - 1)
                else:
                    x_low = jnp.where(row == 0, below[line, :], pltpu.roll(tile(tiles - 1), 1, 0))
                if j < tiles - 1:
                    x_high = tile(j + 1)
                else:
                    x_high = jnp.where(row == 7, above[line, :], pltpu.roll(tile(0), 7, 0))
                left = other_ref[z, rows_at, pl.ds(LANES * (c - 1), LANES)] if c else 0.0
                right = other_ref[z, rows_at, pl.ds(LANES * (c + 1), LANES)] if c < count - 1 else 0.0
                y_low = pltpu.roll(jnp.where(lane == LANES - 1, left, mid), 1, 1)
                y_high = pltpu.roll(jnp.where(lane == 0, right, mid), LANES - 1, 1)
                charge = charge_ref[z, rows_at, at]
                beside = z_low + z_high + mid + jnp.where(first_row, x_low, x_high) + y_low + y_high
                own = own_ref[z, rows_at, at]
                put(z, j, c, jnp.where(charge < PINNED, 0.25 * (beside + charge) - 0.5 * own, own))


def line_scratch(planes, columns):
    return [pltpu.VMEM((planes // 2 * columns // LANES, LANES), jnp.float32)] * 2


def relax_kernel(colour, own_ref, other_ref, charge_ref, ze_ref, xo_ref, xe_ref, zi_ref, after,
                 out_ref, ze_out, xo_out, xe_out, zi_out, below, above):
    del after

    def put(z, j, c, value):
        out_ref[z, pl.ds(8 * j, 8), pl.ds(LANES * c, LANES)] = value

    relax(own_ref, other_ref, charge_ref, ze_ref, xo_ref, xe_ref, zi_ref, below, above, colour, put)
    sends(out_ref, colour, *position()[:2], ze_out, xo_out, xe_out, zi_out)


def half_sweep(own, other, charge, halos, colour, after):
    return pl.pallas_call(
        functools.partial(relax_kernel, colour),
        in_specs=[vmem()] * 7 + [anywhere()],
        out_specs=[vmem()] * 5,
        out_shape=[shape_of(*own.shape)] + send_shapes(*own.shape),
        scratch_shapes=line_scratch(own.shape[0], own.shape[2]),
        compiler_params=params(),
        cost_estimate=cost(14 * own.size, 0),
        name="relax",
    )(own, other, charge, *halos, after)


def split(value):
    high = value.astype(jnp.bfloat16)
    return high, (value - high.astype(jnp.float32)).astype(jnp.bfloat16)


def angles_kernel(rows_total, tiles, columns, offset, after, left_ref, radial_ref, done_ref, terms_ref):
    del after
    done_ref[...] = jnp.zeros_like(done_ref)
    shape = (8, columns)
    column = lax.broadcasted_iota(jnp.int32, shape, 1)
    v = (column.astype(jnp.float32) + 0.5) * (2.0 / columns) - 1.0
    for j in range(tiles):
        packed = lax.broadcasted_iota(jnp.int32, shape, 0) * tiles + j
        row = lax.axis_index("gx") * (16 * tiles) + 2 * packed + (column + offset) % 2
        u = (row.astype(jnp.float32) + 0.5) * (2.0 / rows_total) - 1.0
        inverse = lax.rsqrt(u * u + v * v)
        c1, s1 = u * inverse, v * inverse
        c2, s2 = c1 * c1 - s1 * s1, 2.0 * (c1 * s1)
        c4, s4 = c2 * c2 - s2 * s2, 2.0 * (c2 * s2)
        u2, v2 = u * c1 - v * s1, u * s1 + v * c1
        u3, v3 = u2 * c1 - v2 * s1, u2 * s1 + v2 * c1
        u4, v4 = u2 * c2 - v2 * s2, u2 * s2 + v2 * c2
        for m, value in enumerate((u, u2, u3, u4, v, v2, v3, v4)):
            radial_ref[j, pl.ds(8 * m, 8), :] = value

        def put(index, pair):
            high, low = split(jnp.concatenate(pair, axis=0))
            terms_ref[pl.ds(8 * index, 16), :] = high
            terms_ref[pl.ds(8 * (2 * TURNS + index), 16), :] = low

        twice = 2.0 * c4
        cosines, sines = [jnp.ones_like(c4), c4], [jnp.zeros_like(c4), s4]
        for a in range(0, TURNS, 2):
            put(a, cosines)
            put(TURNS + a, sines)
            for terms in (cosines, sines):
                terms[0] = twice * terms[1] - terms[0]
                terms[1] = twice * terms[0] - terms[1]
        left_ref[j] = terms_ref[...].T


def angles(after, rows_total, tiles, columns, offset):
    left = jax.ShapeDtypeStruct((tiles, columns, 32 * TURNS), jnp.bfloat16)
    return pl.pallas_call(
        functools.partial(angles_kernel, rows_total, tiles, columns, offset),
        in_specs=[anywhere()],
        out_specs=[vmem()] * 3,
        out_shape=[left, shape_of(tiles, 16 * STEPS, columns), shape_of(8, LANES)],
        scratch_shapes=[pltpu.VMEM((32 * TURNS, columns), jnp.bfloat16)],
        compiler_params=params(),
        cost_estimate=cost(128 * tiles * 8 * columns, 0),
        name="angles",
    )(after)


def multipoles_of(colour, field_of, tables, planes, right):
    outs = [None] * planes
    pairs = planes // 2
    n, m = 16 * TURNS, 16 * STEPS * pairs
    tiles = tables[0][0].shape[0]
    for e in (0, 1):
        left_ref, radial_ref = tables[e]
        total = None
        for j in range(tiles):
            slot = (e * tiles + j) % right.shape[0]
            for k in range(pairs):
                f = field_of(2 * k + (e + colour) % 2, j)
                twice = jnp.concatenate([f, f], axis=0)
                for b in range(0, 2 * STEPS, 2):
                    high, low = split(twice * radial_ref[j, pl.ds(8 * b, 16), :])
                    index = 2 * STEPS * k + b
                    right[slot, pl.ds(8 * index, 16), :] = high
                    right[slot, pl.ds(m + 8 * index, 16), :] = low
            product = jnp.dot(right[slot], left_ref[j], preferred_element_type=jnp.float32)
            total = product if total is None else total + product
        total = ((total[:m, :n] + total[m:, :n]) + (total[:m, n:] + total[m:, n:])).T
        i = lax.broadcasted_iota(jnp.int32, total.shape, 0)
        k = lax.broadcasted_iota(jnp.int32, total.shape, 1)
        total = jnp.sum(jnp.where(i % 8 == k % 8, total, 0.0).reshape(2 * TURNS, 8, m), axis=1)
        for shift in (1, 2, 4):
            total = total + pltpu.roll(total, shift, 1)
        half = 8 * STEPS
        even, odd = total[:TURNS], total[TURNS:]
        cosines = even - pltpu.roll(odd, m - half, 1)
        sines = odd + pltpu.roll(even, m - half, 1)
        lane = lax.broadcasted_iota(jnp.int32, (TURNS, m), 1)
        total = jnp.where(lane // half % 2 == 0, cosines, pltpu.roll(sines, half, 1))
        for k in range(pairs):
            outs[2 * k + (e + colour) % 2] = total[:, 2 * half * k : 2 * half * (k + 1)]
    return jnp.concatenate(outs, axis=1)


def right_scratch(planes, columns):
    return pltpu.VMEM((2, 16 * STEPS * planes, columns), jnp.bfloat16)


def sums_shape(planes):
    return shape_of(TURNS, 16 * STEPS * planes)


def multipole_kernel(field_ref, left0, radial0, left1, radial1, out_ref, done_ref, right):
    done_ref[...] = jnp.zeros_like(done_ref)
    out_ref[...] = multipoles_of(
        0,
        lambda z, j: field_ref[z, pl.ds(8 * j, 8), :],
        ((left0, radial0), (left1, radial1)),
        field_ref.shape[0],
        right,
    )


def multipole_sums(field, tables):
    planes, _, columns = field.shape
    return pl.pallas_call(
        multipole_kernel,
        in_specs=[vmem()] * 5,
        out_specs=[vmem()] * 2,
        out_shape=[sums_shape(planes), shape_of(8, LANES)],
        scratch_shapes=[right_scratch(planes, columns)],
        compiler_params=params(),
        cost_estimate=cost(100 * field.size, 0),
        name="multipole",
    )(field, *tables)


def last_kernel(scale, own_ref, other_ref, charge_ref, ze_ref, xo_ref, xe_ref, zi_ref, left0, radial0, left1,
                radial1, sums_ref, after, field_hbm, out_ref, one, staged, right, below, above, sems):
    del after
    planes, rows, columns = own_ref.shape
    tiles = rows // 8
    copies = []

    def put(z, j, c, value):
        at = pl.ds(LANES * c, LANES)
        one[z, pl.ds(8 * j, 8), at] = value
        even = column_parity(8, LANES) == z % 2
        zero = other_ref[z, pl.ds(8 * j, 8), at]
        staged[z, c, pl.ds(2 * j, 8, stride=2 * tiles), :] = jnp.where(even, zero, value)
        staged[z, c, pl.ds(2 * j + 1, 8, stride=2 * tiles), :] = jnp.where(even, value, zero)
        if j == tiles - 1:
            copy = pltpu.make_async_copy(staged.at[z, c], field_hbm.at[z, :, at], sems.at[z, c])
            copy.start()
            copies.append(copy)

    relax(own_ref, other_ref, charge_ref, ze_ref, xo_ref, xe_ref, zi_ref, below, above, 1, put)
    sums = multipoles_of(
        1, lambda z, j: one[z, pl.ds(8 * j, 8), :], ((left0, radial0), (left1, radial1)), planes, right
    )
    out_ref[...] = (sums + sums_ref[...]) * scale
    for copy in copies:
        copy.wait()


def last_half_sweep(own, other, charge, halos, tables, sums, after, scale):
    planes, rows, columns = own.shape
    return pl.pallas_call(
        functools.partial(last_kernel, scale),
        in_specs=[vmem()] * 12 + [anywhere()],
        out_specs=[hbm(), vmem()],
        out_shape=[shape_of(planes, 2 * rows, columns), sums_shape(planes)],
        scratch_shapes=[
            pltpu.VMEM(own.shape, jnp.float32),
            pltpu.VMEM((planes, columns // LANES, 2 * rows, LANES), jnp.float32),
            right_scratch(planes, columns),
            *line_scratch(planes, columns),
            pltpu.SemaphoreType.DMA((planes, columns // LANES)),
        ],
        compiler_params=params(),
        cost_estimate=cost(100 * own.size, 0),
        name="relax_last",
    )(own, other, charge, *halos, *tables, sums, after)


def swaps(pairs):
    return [(a, b) for a, b in pairs] + [(b, a) for a, b in pairs]


def far_pairs(nx, nz):
    step = nx // 4
    pairs = [(x * nz + z, x * nz + z + 1) for x in range(nx) for z in range(1, nz - 1, 2)]
    ends = [x for x in range(nx) if x // step % 2 == 0]
    return swaps(pairs + [(x * nz + z, (x + step) * nz + z) for x in ends for z in (0, nz - 1)])


def odd_pairs(nx, nz):
    pairs = [(x * nz + z, (x + 1) * nz + z) for x in range(1, nx - 1, 2) for z in range(nz)]
    return swaps(pairs + [(x * nz + z, x * nz + z + 1) for x in (0, nx - 1) for z in range(0, nz, 2)])


def local(potential, regions, charge, levels):
    planes, row_count, columns = potential.shape
    nx, nz = lax.axis_size("gx"), lax.axis_size("gz")
    rows_total = nx * row_count
    tiles = row_count // 16
    z_near, x_even = [(i, i ^ 1) for i in range(nz)], [(i, i ^ 1) for i in range(nx)]
    z_far, x_odd = far_pairs(nx, nz), odd_pairs(nx, nz)

    def exchange(ze, xo, xe, zi):
        ze = lax.ppermute(ze, ("gx", "gz"), z_far)
        xo = lax.ppermute(xo, ("gx", "gz"), x_odd)
        xe = lax.ppermute(xe, "gx", x_even)
        zi = lax.ppermute(zi, "gz", z_near)
        return ze, xo, xe, zi

    zero, one, *rest = pack(potential, regions, levels)
    marks, out = rest[:2], rest[2:]
    charge0, charge1, after = pack_charge(charge, marks, out[1])
    tables = []
    for sweep in range(SWEEPS):
        halos = exchange(*out)
        zero, *out = half_sweep(zero, one, charge0, halos, 0, after)
        halos = exchange(*out)
        after = zero
        if sweep < SWEEPS - 1:
            if sweep < 2:
                *table, after = angles(out[1], rows_total, tiles, columns, sweep)
                tables += table
            one, *out = half_sweep(one, zero, charge1, halos, 1, after)
            after = one
    sums, after = multipole_sums(zero, tables)
    scale = 1.0 / math.sqrt(rows_total * columns)
    field, sums = last_half_sweep(one, zero, charge1, halos, tables, sums, after, scale)
    share = K // nx
    parts = jnp.transpose(sums[:, 7::8].reshape(TURNS, planes, 2, STEPS), (1, 2, 0, 3)).reshape(planes, nx, share)
    parts = jnp.transpose(parts, (1, 0, 2)).reshape(nx, planes * share)
    shares = lax.all_to_all(parts, "gx", 0, 0, tiled=True)
    return field, jnp.sum(shares, axis=0).reshape(planes, share)


def solution(mesh):
    in_specs = (P("gz", "gx", None), P("gz", "gx", None), P("gz", "gx", None), P())
    out_specs = (P("gz", "gx", None), P("gz", "gx"))
    return jax.shard_map(local, mesh=mesh, in_specs=in_specs, out_specs=out_specs, check_vma=False)
```

```python
import functools
import math

import jax
import jax.numpy as jnp
from jax import lax
from jax.experimental import pallas as pl
from jax.experimental.pallas import tpu as pltpu
from jax.sharding import PartitionSpec as P

K = 64
SWEEPS = 4
HALF = K // 2
TURNS = 8
STEPS = 4
LANES = 128
PARTS = 1
PITCH = 9
PINNED = 1e30
VMEM_BYTES = 16 * 1024 * 1024
PACK_VMEM_BYTES = 51 * 1024 * 1024
REST_VMEM_BYTES = 46 * 1024 * 1024


def vmem():
    return pl.BlockSpec(memory_space=pltpu.VMEM)


def smem():
    return pl.BlockSpec(memory_space=pltpu.SMEM)


def hbm():
    return pl.BlockSpec(memory_space=pltpu.HBM)


def anywhere():
    return pl.BlockSpec(memory_space=pl.ANY)


def params():
    return pltpu.CompilerParams(vmem_limit_bytes=VMEM_BYTES)


def cost(flops, nbytes):
    return pl.CostEstimate(flops=flops, bytes_accessed=nbytes, transcendentals=0)


def shape_of(*shape):
    return jax.ShapeDtypeStruct(shape, jnp.float32)


def column_parity(rows, columns):
    return lax.broadcasted_iota(jnp.int32, (rows, columns), 1) % 2


def chunks(columns):
    return [(c, pl.ds(LANES * c, LANES)) for c in range(columns // LANES)]


def position():
    gx, gz = lax.axis_index("gx"), lax.axis_index("gz")
    nx, nz = lax.axis_size("gx"), lax.axis_size("gz")
    core = gz % 2
    far = jnp.where(core == 0, gz > 0, gz < nz - 1)
    return core, gx % 2, far, gx > 0, gx < nx - 1


def sends(ref, colour, core, odd, ze_ref, xo_ref, xe_ref, zi_ref):
    planes, rows, columns = ref.shape
    count = columns // LANES
    parity = column_parity(8, LANES)

    def sides(low_ref, high_ref, above_ref, below_ref):
        for j in range(0, rows, 8):
            for _, at in chunks(columns):
                low_ref[pl.ds(j, 8), at] = ref[0, pl.ds(j, 8), at]
                high_ref[pl.ds(j, 8), at] = ref[planes - 1, pl.ds(j, 8), at]
        for k in range(planes // 2):
            for c, at in chunks(columns):
                line = pl.ds(k * count + c, 1)
                last = [ref[2 * k + i, pl.ds(rows - 8, 8), at] for i in (0, 1)]
                first = [ref[2 * k + i, pl.ds(0, 8), at] for i in (0, 1)]
                above_ref[line, :] = jnp.where(parity == 1 - colour, last[0], last[1])[7:8]
                below_ref[line, :] = jnp.where(parity == colour, first[0], first[1])[0:1]

    for c in (0, 1):
        for o in (0, 1):

            @pl.when((core == c) & (odd == o))
            def _():
                z_refs = (zi_ref, ze_ref) if c else (ze_ref, zi_ref)
                x_refs = (xo_ref, xe_ref) if o else (xe_ref, xo_ref)
                sides(*z_refs, *x_refs)


def spread_rows(source, tiles, even, wanted):
    for j in wanted:
        a = source[pl.ds(2 * j, 8, stride=2 * tiles), :]
        b = source[pl.ds(2 * j + 1, 8, stride=2 * tiles), :]
        yield pl.ds(8 * j, 8), jnp.where(even, a, b), jnp.where(even, b, a)


def level_table(lev_ref):
    lane = lax.broadcasted_iota(jnp.int32, (8, LANES), 1)
    table = jnp.zeros((8, LANES), jnp.float32)
    for region in range(1, lev_ref.shape[0]):
        table = jnp.where(lane == region, lev_ref[region], table)
    return table


def start_field(table, reg_ref, pot_ref, z, j, at):
    region = reg_ref[z, pl.ds(j, 8), at]
    pinned = jnp.take_along_axis(table, region, axis=1)
    free = region == 0
    return jnp.where(free, pot_ref[z, pl.ds(j, 8), at], pinned), jnp.where(free, 0.0, PINNED)


def pack_kernel(pot_hbm, reg_hbm, lev_hbm, f0_ref, f1_ref, m0_ref, m1_ref, ze_ref, xo_ref, xe_ref, zi_ref, lev_ref,
                pot_ref, reg_ref, field, mark, one, lev_sem, sems):
    planes, rows, columns = one.shape
    tiles = rows // 8
    lev_copy = pltpu.make_async_copy(lev_hbm, lev_ref, lev_sem)
    lev_copy.start()
    parts = {z: ((0, 2 * rows),) if z in (0, planes - 1) else ((0, 8), (2 * rows - 8, 8)) for z in range(planes)}
    order = sorted(parts, key=lambda z: len(parts[z]))
    copies = {
        z: [
            pltpu.make_async_copy(source.at[z, pl.ds(j, size)], target.at[z, pl.ds(j, size)], sems.at[z, i, k])
            for k, (j, size) in enumerate(parts[z])
            for i, (source, target) in enumerate(((reg_hbm, reg_ref), (pot_hbm, pot_ref)))
        ]
        for z in order
    }
    for z in order:
        for copy in copies[z]:
            copy.start()
    lev_copy.wait()
    table = level_table(lev_ref)
    for z in order:
        even = column_parity(8, LANES) == z % 2
        for copy in copies[z]:
            copy.wait()
        whole = z in (0, planes - 1)
        for c, at in chunks(columns):
            slot = z % 2 * (columns // LANES) + c
            for first, size in parts[z]:
                for j in range(first, first + size, 8):
                    field[slot, pl.ds(j, 8), :], mark[slot, pl.ds(j, 8), :] = start_field(
                        table, reg_ref, pot_ref, z, j, at
                    )
            for to, a, b in spread_rows(field.at[slot], tiles, even, range(tiles) if whole else (0, tiles - 1)):
                one[z, to, at] = b
                if whole:
                    f0_ref[z // (planes - 1), to, at] = a
                    f1_ref[z // (planes - 1), to, at] = b
            if whole:
                for to, a, b in spread_rows(mark.at[slot], tiles, even, range(tiles)):
                    m0_ref[z // (planes - 1), to, at] = a
                    m1_ref[z // (planes - 1), to, at] = b
    sends(one, 1, *position()[:2], ze_ref, xo_ref, xe_ref, zi_ref)


def send_shapes(planes, rows, columns):
    side, line = shape_of(rows, columns), shape_of(planes // 2 * columns // LANES, LANES)
    return [side, line, line, side]


def pack(potential, regions, levels):
    planes, rows, columns = potential.shape
    half = shape_of(planes, rows // 2, columns)
    whole = (planes, rows, columns)
    stage = pltpu.VMEM((2 * columns // LANES, rows, LANES), jnp.float32)
    return pl.pallas_call(
        pack_kernel,
        in_specs=[hbm()] * 3,
        out_specs=[vmem()] * 8,
        out_shape=[shape_of(2, *half.shape[1:])] * 4 + send_shapes(*half.shape),
        scratch_shapes=[
            pltpu.SMEM(levels.shape, jnp.float32),
            pltpu.VMEM(whole, jnp.float32),
            pltpu.VMEM(whole, jnp.int32),
            stage,
            stage,
            pltpu.VMEM(half.shape, jnp.float32),
            pltpu.SemaphoreType.DMA,
            pltpu.SemaphoreType.DMA((planes, 2, 2)),
        ],
        compiler_params=pltpu.CompilerParams(vmem_limit_bytes=PACK_VMEM_BYTES),
        cost_estimate=cost(20 * potential.size, 8 * potential.size),
        name="pack",
    )(potential, regions, levels)


def rest_kernel(pot_hbm, reg_hbm, chg_hbm, lev_hbm, f0_ref, f1_ref, m0_ref, m1_ref, after, zero_ref, one_ref, c0_ref,
                c1_ref, done_ref, lev_ref, pot_ref, reg_ref, chg_ref, field, stage, lev_sem, sems):
    del after
    done_ref[...] = jnp.zeros_like(done_ref)
    planes, rows, columns = zero_ref.shape
    tiles = rows // 8
    lev_copy = pltpu.make_async_copy(lev_hbm, lev_ref, lev_sem)
    lev_copy.start()
    inner = range(1, planes - 1)
    order = [*inner, 0, planes - 1]
    copies = {}
    for z in order:
        pairs = ((reg_hbm, reg_ref), (pot_hbm, pot_ref), (chg_hbm, chg_ref))
        copies[z] = [
            pltpu.make_async_copy(source.at[z], target.at[z], sems.at[z, i])
            for i, (source, target) in enumerate(pairs)
            if z in inner or i == 2
        ]
        for copy in copies[z]:
            copy.start()
    lev_copy.wait()
    table = level_table(lev_ref)
    for z in (0, planes - 1):
        zero_ref[z] = f0_ref[z // (planes - 1)]
        one_ref[z] = f1_ref[z // (planes - 1)]
    for z in order:
        even = column_parity(8, LANES) == z % 2
        for copy in copies[z]:
            copy.wait()
        for c, at in chunks(columns):
            slot = z % 2 * (columns // LANES) + c
            for j in range(0, 2 * rows, 8):
                charge = chg_ref[z, pl.ds(j, 8), at]
                if z in inner:
                    field[slot, pl.ds(j, 8), :], mark = start_field(table, reg_ref, pot_ref, z, j, at)
                    charge = charge + mark
                stage[slot, pl.ds(j, 8), :] = charge
            for to, a, b in spread_rows(stage.at[slot], tiles, even, range(tiles)):
                c0_ref[z, to, at] = a if z in inner else m0_ref[z // (planes - 1), to, at] + a
                c1_ref[z, to, at] = b if z in inner else m1_ref[z // (planes - 1), to, at] + b
            if z in inner:
                for to, a, b in spread_rows(field.at[slot], tiles, even, range(tiles)):
                    zero_ref[z, to, at] = a
                    one_ref[z, to, at] = b


def pack_rest(potential, regions, charge, levels, packed, after):
    planes, rows, columns = charge.shape
    half = shape_of(planes, rows // 2, columns)
    stage = pltpu.VMEM((2 * columns // LANES, rows, LANES), jnp.float32)
    return pl.pallas_call(
        rest_kernel,
        in_specs=[hbm()] * 4 + [vmem()] * 4 + [anywhere()],
        out_specs=[vmem()] * 5,
        out_shape=[half] * 4 + [shape_of(8, LANES)],
        scratch_shapes=[
            pltpu.SMEM(levels.shape, jnp.float32),
            pltpu.VMEM(charge.shape, jnp.float32),
            pltpu.VMEM(charge.shape, jnp.int32),
            pltpu.VMEM(charge.shape, jnp.float32),
            stage,
            stage,
            pltpu.SemaphoreType.DMA,
            pltpu.SemaphoreType.DMA((planes, 3)),
        ],
        compiler_params=pltpu.CompilerParams(vmem_limit_bytes=REST_VMEM_BYTES),
        cost_estimate=cost(40 * charge.size, 8 * charge.size),
        name="pack_rest",
    )(potential, regions, charge, levels, *packed, after)


def relax(own_ref, other_ref, charge_ref, ze_ref, xo_ref, xe_ref, zi_ref, below, above, colour, put):
    core, odd, far_live, below_live, above_live = position()
    planes, rows, columns = own_ref.shape
    tiles, count = rows // 8, columns // LANES
    row = lax.broadcasted_iota(jnp.int32, (8, LANES), 0)
    lane = lax.broadcasted_iota(jnp.int32, (8, LANES), 1)
    parity = column_parity(8, LANES)
    xe, xo = xe_ref[...], xo_ref[...]
    below[...] = jnp.where(below_live, jnp.where(odd == 0, xo, xe), 0.0)
    above[...] = jnp.where(above_live, jnp.where(odd == 0, xe, xo), 0.0)

    def tile_step(z, j):
        first_row = parity == (z + colour) % 2
        rows_at = pl.ds(8 * j, 8)
        for c, at in chunks(columns):
            tile = lambda t, at=at: other_ref[z, pl.ds(8 * t, 8), at]
            mid = tile(j)
            if z in (0, planes - 1):
                far = jnp.where(far_live, ze_ref[rows_at, at], 0.0)
                near = zi_ref[rows_at, at]
            z_low = other_ref[z - 1, rows_at, at] if z else jnp.where(core == 0, far, near)
            z_high = other_ref[z + 1, rows_at, at] if z < planes - 1 else jnp.where(core == 0, near, far)
            line = pl.ds(z // 2 * count + c, 1)
            if j:
                x_low = tile(j - 1)
            else:
                x_low = jnp.where(row == 0, below[line, :], pltpu.roll(tile(tiles - 1), 1, 0))
            if j < tiles - 1:
                x_high = tile(j + 1)
            else:
                x_high = jnp.where(row == 7, above[line, :], pltpu.roll(tile(0), 7, 0))
            left = other_ref[z, rows_at, pl.ds(LANES * (c - 1), LANES)] if c else 0.0
            right = other_ref[z, rows_at, pl.ds(LANES * (c + 1), LANES)] if c < count - 1 else 0.0
            y_low = pltpu.roll(jnp.where(lane == LANES - 1, left, mid), 1, 1)
            y_high = pltpu.roll(jnp.where(lane == 0, right, mid), LANES - 1, 1)
            charge = charge_ref[z, rows_at, at]
            beside = z_low + z_high + mid + jnp.where(first_row, x_low, x_high) + y_low + y_high
            own = own_ref[z, rows_at, at]
            put(z, j, c, jnp.where(charge < PINNED, 0.25 * (beside + charge) - 0.5 * own, own))

    return tile_step


def line_scratch(planes, columns):
    return [pltpu.VMEM((planes // 2 * columns // LANES, LANES), jnp.float32)] * 2


def relax_kernel(colour, own_ref, other_ref, charge_ref, ze_ref, xo_ref, xe_ref, zi_ref, after,
                 out_ref, ze_out, xo_out, xe_out, zi_out, below, above):
    del after

    def put(z, j, c, value):
        out_ref[z, pl.ds(8 * j, 8), pl.ds(LANES * c, LANES)] = value

    step = relax(own_ref, other_ref, charge_ref, ze_ref, xo_ref, xe_ref, zi_ref, below, above, colour, put)
    for z in range(own_ref.shape[0]):
        for j in range(own_ref.shape[1] // 8):
            step(z, j)
    sends(out_ref, colour, *position()[:2], ze_out, xo_out, xe_out, zi_out)


def half_sweep(own, other, charge, halos, colour, after):
    return pl.pallas_call(
        functools.partial(relax_kernel, colour),
        in_specs=[vmem()] * 7 + [anywhere()],
        out_specs=[vmem()] * 5,
        out_shape=[shape_of(*own.shape)] + send_shapes(*own.shape),
        scratch_shapes=line_scratch(own.shape[0], own.shape[2]),
        compiler_params=params(),
        cost_estimate=cost(14 * own.size, 0),
        name="relax",
    )(own, other, charge, *halos, after)


def split(value):
    high = value.astype(jnp.bfloat16)
    return high, (value - high.astype(jnp.float32)).astype(jnp.bfloat16)


def angles_kernel(rows_total, tiles, columns, offset, after, left_ref, radial_ref, done_ref, terms_ref):
    del after
    done_ref[...] = jnp.zeros_like(done_ref)
    shape = (8, columns)
    column = lax.broadcasted_iota(jnp.int32, shape, 1)
    v = (column.astype(jnp.float32) + 0.5) * (2.0 / columns) - 1.0
    for j in range(tiles):
        packed = lax.broadcasted_iota(jnp.int32, shape, 0) * tiles + j
        row = lax.axis_index("gx") * (16 * tiles) + 2 * packed + (column + offset) % 2
        u = (row.astype(jnp.float32) + 0.5) * (2.0 / rows_total) - 1.0
        inverse = lax.rsqrt(u * u + v * v)
        c1, s1 = u * inverse, v * inverse
        c2, s2 = c1 * c1 - s1 * s1, 2.0 * (c1 * s1)
        c4, s4 = c2 * c2 - s2 * s2, 2.0 * (c2 * s2)
        u2, v2 = u * c1 - v * s1, u * s1 + v * c1
        u3, v3 = u2 * c1 - v2 * s1, u2 * s1 + v2 * c1
        u4, v4 = u2 * c2 - v2 * s2, u2 * s2 + v2 * c2
        for m, value in enumerate((u, u2, u3, u4, v, v2, v3, v4)):
            radial_ref[j, pl.ds(8 * m, 8), :] = value

        def put(index, pair):
            high, low = split(jnp.concatenate(pair, axis=0))
            terms_ref[pl.ds(8 * index, 16), :] = high
            terms_ref[pl.ds(8 * (2 * TURNS + index), 16), :] = low

        twice = 2.0 * c4
        cosines, sines = [jnp.ones_like(c4), c4], [jnp.zeros_like(c4), s4]
        for a in range(0, TURNS, 2):
            put(a, cosines)
            put(TURNS + a, sines)
            for terms in (cosines, sines):
                terms[0] = twice * terms[1] - terms[0]
                terms[1] = twice * terms[0] - terms[1]
        left_ref[j] = terms_ref[...].T


def angles(after, rows_total, tiles, columns, offset):
    left = jax.ShapeDtypeStruct((tiles, columns, 32 * TURNS), jnp.bfloat16)
    return pl.pallas_call(
        functools.partial(angles_kernel, rows_total, tiles, columns, offset),
        in_specs=[anywhere()],
        out_specs=[vmem()] * 3,
        out_shape=[left, shape_of(tiles, 16 * STEPS, columns), shape_of(8, LANES)],
        scratch_shapes=[pltpu.VMEM((32 * TURNS, columns), jnp.bfloat16)],
        compiler_params=params(),
        cost_estimate=cost(128 * tiles * 8 * columns, 0),
        name="angles",
    )(after)


def multipoles_of(colour, field_of, tables, planes, right):
    outs = [None] * planes
    pairs = planes // 2
    n, m = 16 * TURNS, 16 * STEPS * pairs
    tiles = tables[0][0].shape[0]
    totals = [None, None]

    def add_tile(e, j):
        left_ref, radial_ref = tables[e]
        slot = (e * tiles + j) % right.shape[0]
        for k in range(pairs):
            f = field_of(2 * k + (e + colour) % 2, j)
            twice = jnp.concatenate([f, f], axis=0)
            for b in range(0, 2 * STEPS, 2):
                high, low = split(twice * radial_ref[j, pl.ds(8 * b, 16), :])
                index = 2 * STEPS * k + b
                right[slot, pl.ds(8 * index, 16), :] = high
                right[slot, pl.ds(m + 8 * index, 16), :] = low
        product = jnp.dot(right[slot], left_ref[j], preferred_element_type=jnp.float32)
        totals[e] = product if totals[e] is None else totals[e] + product

    def finish():
        for e in (0, 1):
            total = totals[e]
            total = ((total[:m, :n] + total[m:, :n]) + (total[:m, n:] + total[m:, n:])).T
            i = lax.broadcasted_iota(jnp.int32, total.shape, 0)
            k = lax.broadcasted_iota(jnp.int32, total.shape, 1)
            total = jnp.sum(jnp.where(i % 8 == k % 8, total, 0.0).reshape(2 * TURNS, 8, m), axis=1)
            for shift in (1, 2, 4):
                total = total + pltpu.roll(total, shift, 1)
            half = 8 * STEPS
            even, odd = total[:TURNS], total[TURNS:]
            cosines = even - pltpu.roll(odd, m - half, 1)
            sines = odd + pltpu.roll(even, m - half, 1)
            lane = lax.broadcasted_iota(jnp.int32, (TURNS, m), 1)
            total = jnp.where(lane // half % 2 == 0, cosines, pltpu.roll(sines, half, 1))
            for k in range(pairs):
                outs[2 * k + (e + colour) % 2] = total[:, 2 * half * k : 2 * half * (k + 1)]
        return jnp.concatenate(outs, axis=1)

    return add_tile, finish


def right_scratch(planes, columns):
    return pltpu.VMEM((2, 16 * STEPS * planes, columns), jnp.bfloat16)


def sums_shape(planes):
    return shape_of(TURNS, 16 * STEPS * planes)


def multipole_kernel(field_ref, left0, radial0, left1, radial1, out_ref, done_ref, right):
    done_ref[...] = jnp.zeros_like(done_ref)
    planes, rows, _ = field_ref.shape
    add_tile, finish = multipoles_of(
        0, lambda z, j: field_ref[z, pl.ds(8 * j, 8), :], ((left0, radial0), (left1, radial1)), planes, right
    )
    for e in (0, 1):
        for j in range(rows // 8):
            add_tile(e, j)
    out_ref[...] = finish()


def multipole_sums(field, tables):
    planes, _, columns = field.shape
    return pl.pallas_call(
        multipole_kernel,
        in_specs=[vmem()] * 5,
        out_specs=[vmem()] * 2,
        out_shape=[sums_shape(planes), shape_of(8, LANES)],
        scratch_shapes=[right_scratch(planes, columns)],
        compiler_params=params(),
        cost_estimate=cost(100 * field.size, 0),
        name="multipole",
    )(field, *tables)


def last_kernel(scale, own_ref, other_ref, charge_ref, ze_ref, xo_ref, xe_ref, zi_ref, left0, radial0, left1,
                radial1, sums_ref, after, field_hbm, out_ref, one, staged, right, below, above, sems):
    del after
    planes, rows, columns = own_ref.shape
    tiles = rows // 8
    copies = []

    def put(z, j, c, value):
        at = pl.ds(LANES * c, LANES)
        one[z, pl.ds(8 * j, 8), at] = value
        even = column_parity(8, LANES) == z % 2
        zero = other_ref[z, pl.ds(8 * j, 8), at]
        staged[z, c, pl.ds(2 * j, 8, stride=2 * tiles), :] = jnp.where(even, zero, value)
        staged[z, c, pl.ds(2 * j + 1, 8, stride=2 * tiles), :] = jnp.where(even, value, zero)
        if j == tiles - 1:
            copy = pltpu.make_async_copy(staged.at[z, c], field_hbm.at[z, :, at], sems.at[z, c])
            copy.start()
            copies.append(copy)

    relax_tile = relax(own_ref, other_ref, charge_ref, ze_ref, xo_ref, xe_ref, zi_ref, below, above, 1, put)
    add_tile, finish = multipoles_of(
        1, lambda z, j: one[z, pl.ds(8 * j, 8), :], ((left0, radial0), (left1, radial1)), planes, right
    )
    for z in range(1, planes, 2):
        for j in range(tiles):
            relax_tile(z, j)
    for j in range(tiles):
        add_tile(0, j)
        for z in range(0, planes, 2):
            relax_tile(z, j)
    for j in range(tiles):
        add_tile(1, j)
    out_ref[...] = (finish() + sums_ref[...]) * scale
    for copy in copies:
        copy.wait()


def last_half_sweep(own, other, charge, halos, tables, sums, after, scale):
    planes, rows, columns = own.shape
    return pl.pallas_call(
        functools.partial(last_kernel, scale),
        in_specs=[vmem()] * 12 + [anywhere()],
        out_specs=[hbm(), vmem()],
        out_shape=[shape_of(planes, 2 * rows, columns), sums_shape(planes)],
        scratch_shapes=[
            pltpu.VMEM(own.shape, jnp.float32),
            pltpu.VMEM((planes, columns // LANES, 2 * rows, LANES), jnp.float32),
            right_scratch(planes, columns),
            *line_scratch(planes, columns),
            pltpu.SemaphoreType.DMA((planes, columns // LANES)),
        ],
        compiler_params=params(),
        cost_estimate=cost(100 * own.size, 0),
        name="relax_last",
    )(own, other, charge, *halos, *tables, sums, after)


def swaps(pairs):
    return [(a, b) for a, b in pairs] + [(b, a) for a, b in pairs]


def far_pairs(nx, nz):
    step = nx // 4
    pairs = [(x * nz + z, x * nz + z + 1) for x in range(nx) for z in range(1, nz - 1, 2)]
    ends = [x for x in range(nx) if x // step % 2 == 0]
    return swaps(pairs + [(x * nz + z, (x + step) * nz + z) for x in ends for z in (0, nz - 1)])


def odd_pairs(nx, nz):
    pairs = [(x * nz + z, (x + 1) * nz + z) for x in range(1, nx - 1, 2) for z in range(nz)]
    return swaps(pairs + [(x * nz + z, x * nz + z + 1) for x in (0, nx - 1) for z in range(0, nz, 2)])


def local(potential, regions, charge, levels):
    planes, row_count, columns = potential.shape
    nx, nz = lax.axis_size("gx"), lax.axis_size("gz")
    rows_total = nx * row_count
    tiles = row_count // 16
    z_near, x_even = [(i, i ^ 1) for i in range(nz)], [(i, i ^ 1) for i in range(nx)]
    z_far, x_odd = far_pairs(nx, nz), odd_pairs(nx, nz)

    def exchange(ze, xo, xe, zi):
        ze = lax.ppermute(ze, ("gx", "gz"), z_far)
        xo = lax.ppermute(xo, ("gx", "gz"), x_odd)
        xe = lax.ppermute(xe, "gx", x_even)
        zi = lax.ppermute(zi, "gz", z_near)
        return ze, xo, xe, zi

    *packed, ze, xo, xe, zi = pack(potential, regions, levels)
    out = ze, xo, xe, zi
    zero, one, charge0, charge1, after = pack_rest(potential, regions, charge, levels, packed, xo)
    tables = []
    for sweep in range(SWEEPS):
        halos = exchange(*out)
        zero, *out = half_sweep(zero, one, charge0, halos, 0, after)
        halos = exchange(*out)
        after = zero
        if sweep < SWEEPS - 1:
            if sweep < 2:
                *table, after = angles(out[1], rows_total, tiles, columns, sweep)
                tables += table
            one, *out = half_sweep(one, zero, charge1, halos, 1, after)
            after = one
    sums, after = multipole_sums(zero, tables)
    scale = 1.0 / math.sqrt(rows_total * columns)
    field, sums = last_half_sweep(one, zero, charge1, halos, tables, sums, after, scale)
    share = K // nx
    parts = jnp.transpose(sums[:, 7::8].reshape(TURNS, planes, 2, STEPS), (1, 2, 0, 3)).reshape(planes, nx, share)
    parts = jnp.transpose(parts, (1, 0, 2)).reshape(nx, planes * share)
    shares = lax.all_to_all(parts, "gx", 0, 0, tiled=True)
    return field, jnp.sum(shares, axis=0).reshape(planes, share)


def solution(mesh):
    in_specs = (P("gz", "gx", None), P("gz", "gx", None), P("gz", "gx", None), P())
    out_specs = (P("gz", "gx", None), P("gz", "gx"))
    return jax.shard_map(local, mesh=mesh, in_specs=in_specs, out_specs=out_specs, check_vma=False)
```

```python
import functools
import math

import jax
import jax.numpy as jnp
from jax import lax
from jax.experimental import pallas as pl
from jax.experimental.pallas import tpu as pltpu
from jax.sharding import PartitionSpec as P

K = 64
SWEEPS = 4
HALF = K // 2
TURNS = 8
STEPS = 4
LANES = 128
PARTS = 1
PITCH = 9
PINNED = 1e30
VMEM_BYTES = 16 * 1024 * 1024
PACK_VMEM_BYTES = 51 * 1024 * 1024
REST_VMEM_BYTES = 46 * 1024 * 1024


def vmem():
    return pl.BlockSpec(memory_space=pltpu.VMEM)


def smem():
    return pl.BlockSpec(memory_space=pltpu.SMEM)


def hbm():
    return pl.BlockSpec(memory_space=pltpu.HBM)


def anywhere():
    return pl.BlockSpec(memory_space=pl.ANY)


def params():
    return pltpu.CompilerParams(vmem_limit_bytes=VMEM_BYTES)


def cost(flops, nbytes):
    return pl.CostEstimate(flops=flops, bytes_accessed=nbytes, transcendentals=0)


def shape_of(*shape):
    return jax.ShapeDtypeStruct(shape, jnp.float32)


def column_parity(rows, columns):
    return lax.broadcasted_iota(jnp.int32, (rows, columns), 1) % 2


def chunks(columns):
    return [(c, pl.ds(LANES * c, LANES)) for c in range(columns // LANES)]


def position():
    gx, gz = lax.axis_index("gx"), lax.axis_index("gz")
    nx, nz = lax.axis_size("gx"), lax.axis_size("gz")
    core = gz % 2
    far = jnp.where(core == 0, gz > 0, gz < nz - 1)
    return core, gx % 2, far, gx > 0, gx < nx - 1


def sends(ref, colour, core, odd, ze_ref, xo_ref, xe_ref, zi_ref):
    planes, rows, columns = ref.shape
    count = columns // LANES
    parity = column_parity(8, LANES)

    def sides(low_ref, high_ref, above_ref, below_ref):
        for j in range(0, rows, 8):
            for _, at in chunks(columns):
                low_ref[pl.ds(j, 8), at] = ref[0, pl.ds(j, 8), at]
                high_ref[pl.ds(j, 8), at] = ref[planes - 1, pl.ds(j, 8), at]
        for k in range(planes // 2):
            for c, at in chunks(columns):
                line = pl.ds(k * count + c, 1)
                last = [ref[2 * k + i, pl.ds(rows - 8, 8), at] for i in (0, 1)]
                first = [ref[2 * k + i, pl.ds(0, 8), at] for i in (0, 1)]
                above_ref[line, :] = jnp.where(parity == 1 - colour, last[0], last[1])[7:8]
                below_ref[line, :] = jnp.where(parity == colour, first[0], first[1])[0:1]

    for c in (0, 1):
        for o in (0, 1):

            @pl.when((core == c) & (odd == o))
            def _():
                z_refs = (zi_ref, ze_ref) if c else (ze_ref, zi_ref)
                x_refs = (xo_ref, xe_ref) if o else (xe_ref, xo_ref)
                sides(*z_refs, *x_refs)


def spread_rows(source, tiles, even, wanted):
    for j in wanted:
        a = source[pl.ds(2 * j, 8, stride=2 * tiles), :]
        b = source[pl.ds(2 * j + 1, 8, stride=2 * tiles), :]
        yield pl.ds(8 * j, 8), jnp.where(even, a, b), jnp.where(even, b, a)


def level_table(lev_ref):
    lane = lax.broadcasted_iota(jnp.int32, (8, LANES), 1)
    table = jnp.zeros((8, LANES), jnp.float32)
    for region in range(1, lev_ref.shape[0]):
        table = jnp.where(lane == region, lev_ref[region], table)
    return table


def start_field(table, reg_ref, pot_ref, z, j, at):
    region = reg_ref[z, pl.ds(j, 8), at]
    pinned = jnp.take_along_axis(table, region, axis=1)
    free = region == 0
    return jnp.where(free, pot_ref[z, pl.ds(j, 8), at], pinned), jnp.where(free, 0.0, PINNED)


def pack_kernel(pot_hbm, reg_hbm, lev_hbm, f0_ref, f1_ref, m0_ref, m1_ref, ze_ref, xo_ref, xe_ref, zi_ref, lev_ref,
                pot_ref, reg_ref, field, mark, one, lev_sem, sems):
    planes, rows, columns = one.shape
    tiles = rows // 8
    lev_copy = pltpu.make_async_copy(lev_hbm, lev_ref, lev_sem)
    lev_copy.start()
    parts = {z: ((0, 2 * rows),) if z in (0, planes - 1) else ((0, 8), (2 * rows - 8, 8)) for z in range(planes)}
    order = sorted(parts, key=lambda z: len(parts[z]))
    copies = {
        z: [
            pltpu.make_async_copy(source.at[z, pl.ds(j, size)], target.at[z, pl.ds(j, size)], sems.at[z, i, k])
            for k, (j, size) in enumerate(parts[z])
            for i, (source, target) in enumerate(((reg_hbm, reg_ref), (pot_hbm, pot_ref)))
        ]
        for z in order
    }
    for z in order:
        for copy in copies[z]:
            copy.start()
    lev_copy.wait()
    table = level_table(lev_ref)
    for z in order:
        even = column_parity(8, LANES) == z % 2
        for copy in copies[z]:
            copy.wait()
        whole = z in (0, planes - 1)
        for c, at in chunks(columns):
            slot = z % 2 * (columns // LANES) + c
            for first, size in parts[z]:
                for j in range(first, first + size, 8):
                    field[slot, pl.ds(j, 8), :], mark[slot, pl.ds(j, 8), :] = start_field(
                        table, reg_ref, pot_ref, z, j, at
                    )
            for to, a, b in spread_rows(field.at[slot], tiles, even, range(tiles) if whole else (0, tiles - 1)):
                one[z, to, at] = b
                if whole:
                    f0_ref[z // (planes - 1), to, at] = a
                    f1_ref[z // (planes - 1), to, at] = b
            if whole:
                for to, a, b in spread_rows(mark.at[slot], tiles, even, range(tiles)):
                    m0_ref[z // (planes - 1), to, at] = a
                    m1_ref[z // (planes - 1), to, at] = b
    sends(one, 1, *position()[:2], ze_ref, xo_ref, xe_ref, zi_ref)


def send_shapes(planes, rows, columns):
    side, line = shape_of(rows, columns), shape_of(planes // 2 * columns // LANES, LANES)
    return [side, line, line, side]


def pack(potential, regions, levels):
    planes, rows, columns = potential.shape
    half = shape_of(planes, rows // 2, columns)
    whole = (planes, rows, columns)
    stage = pltpu.VMEM((2 * columns // LANES, rows, LANES), jnp.float32)
    return pl.pallas_call(
        pack_kernel,
        in_specs=[hbm()] * 3,
        out_specs=[vmem()] * 8,
        out_shape=[shape_of(2, *half.shape[1:])] * 4 + send_shapes(*half.shape),
        scratch_shapes=[
            pltpu.SMEM(levels.shape, jnp.float32),
            pltpu.VMEM(whole, jnp.float32),
            pltpu.VMEM(whole, jnp.int32),
            stage,
            stage,
            pltpu.VMEM(half.shape, jnp.float32),
            pltpu.SemaphoreType.DMA,
            pltpu.SemaphoreType.DMA((planes, 2, 2)),
        ],
        compiler_params=pltpu.CompilerParams(vmem_limit_bytes=PACK_VMEM_BYTES),
        cost_estimate=cost(20 * potential.size, 8 * potential.size),
        name="pack",
    )(potential, regions, levels)


def rest_kernel(pot_hbm, reg_hbm, chg_hbm, lev_hbm, f0_ref, f1_ref, m0_ref, m1_ref, after, zero_ref, one_ref, c0_ref,
                c1_ref, done_ref, lev_ref, pot_ref, reg_ref, chg_ref, field, stage, lev_sem, sems):
    del after
    done_ref[...] = jnp.zeros_like(done_ref)
    planes, rows, columns = zero_ref.shape
    tiles = rows // 8
    lev_copy = pltpu.make_async_copy(lev_hbm, lev_ref, lev_sem)
    lev_copy.start()
    inner = range(1, planes - 1)
    order = [*inner, 0, planes - 1]
    copies = {}
    for z in order:
        pairs = ((reg_hbm, reg_ref), (pot_hbm, pot_ref), (chg_hbm, chg_ref))
        copies[z] = [
            pltpu.make_async_copy(source.at[z], target.at[z], sems.at[z, i])
            for i, (source, target) in enumerate(pairs)
            if z in inner or i == 2
        ]
        for copy in copies[z]:
            copy.start()
    lev_copy.wait()
    table = level_table(lev_ref)
    for z in (0, planes - 1):
        zero_ref[z] = f0_ref[z // (planes - 1)]
        one_ref[z] = f1_ref[z // (planes - 1)]
    for z in order:
        even = column_parity(8, LANES) == z % 2
        for copy in copies[z]:
            copy.wait()
        for c, at in chunks(columns):
            slot = z % 2 * (columns // LANES) + c
            for j in range(0, 2 * rows, 8):
                charge = chg_ref[z, pl.ds(j, 8), at]
                if z in inner:
                    field[slot, pl.ds(j, 8), :], mark = start_field(table, reg_ref, pot_ref, z, j, at)
                    charge = charge + mark
                stage[slot, pl.ds(j, 8), :] = charge
            for to, a, b in spread_rows(stage.at[slot], tiles, even, range(tiles)):
                c0_ref[z, to, at] = a if z in inner else m0_ref[z // (planes - 1), to, at] + a
                c1_ref[z, to, at] = b if z in inner else m1_ref[z // (planes - 1), to, at] + b
            if z in inner:
                for to, a, b in spread_rows(field.at[slot], tiles, even, range(tiles)):
                    zero_ref[z, to, at] = a
                    one_ref[z, to, at] = b


def pack_rest(potential, regions, charge, levels, packed, after):
    planes, rows, columns = charge.shape
    half = shape_of(planes, rows // 2, columns)
    stage = pltpu.VMEM((2 * columns // LANES, rows, LANES), jnp.float32)
    return pl.pallas_call(
        rest_kernel,
        in_specs=[hbm()] * 4 + [vmem()] * 4 + [anywhere()],
        out_specs=[vmem()] * 5,
        out_shape=[half] * 4 + [shape_of(8, LANES)],
        scratch_shapes=[
            pltpu.SMEM(levels.shape, jnp.float32),
            pltpu.VMEM(charge.shape, jnp.float32),
            pltpu.VMEM(charge.shape, jnp.int32),
            pltpu.VMEM(charge.shape, jnp.float32),
            stage,
            stage,
            pltpu.SemaphoreType.DMA,
            pltpu.SemaphoreType.DMA((planes, 3)),
        ],
        compiler_params=pltpu.CompilerParams(vmem_limit_bytes=REST_VMEM_BYTES),
        cost_estimate=cost(40 * charge.size, 8 * charge.size),
        name="pack_rest",
    )(potential, regions, charge, levels, *packed, after)


def relax(own_ref, other_ref, charge_ref, ze_ref, xo_ref, xe_ref, zi_ref, below, above, colour, put):
    core, odd, far_live, below_live, above_live = position()
    planes, rows, columns = own_ref.shape
    tiles, count = rows // 8, columns // LANES
    row = lax.broadcasted_iota(jnp.int32, (8, LANES), 0)
    lane = lax.broadcasted_iota(jnp.int32, (8, LANES), 1)
    parity = column_parity(8, LANES)
    xe, xo = xe_ref[...], xo_ref[...]
    below[...] = jnp.where(below_live, jnp.where(odd == 0, xo, xe), 0.0)
    above[...] = jnp.where(above_live, jnp.where(odd == 0, xe, xo), 0.0)

    def tile_step(z, j):
        first_row = parity == (z + colour) % 2
        rows_at = pl.ds(8 * j, 8)
        for c, at in chunks(columns):
            tile = lambda t, at=at: other_ref[z, pl.ds(8 * t, 8), at]
            mid = tile(j)
            if z in (0, planes - 1):
                far = jnp.where(far_live, ze_ref[rows_at, at], 0.0)
                near = zi_ref[rows_at, at]
            z_low = other_ref[z - 1, rows_at, at] if z else jnp.where(core == 0, far, near)
            z_high = other_ref[z + 1, rows_at, at] if z < planes - 1 else jnp.where(core == 0, near, far)
            line = pl.ds(z // 2 * count + c, 1)
            if j:
                x_low = tile(j - 1)
            else:
                x_low = jnp.where(row == 0, below[line, :], pltpu.roll(tile(tiles - 1), 1, 0))
            if j < tiles - 1:
                x_high = tile(j + 1)
            else:
                x_high = jnp.where(row == 7, above[line, :], pltpu.roll(tile(0), 7, 0))
            left = other_ref[z, rows_at, pl.ds(LANES * (c - 1), LANES)] if c else 0.0
            right = other_ref[z, rows_at, pl.ds(LANES * (c + 1), LANES)] if c < count - 1 else 0.0
            y_low = pltpu.roll(jnp.where(lane == LANES - 1, left, mid), 1, 1)
            y_high = pltpu.roll(jnp.where(lane == 0, right, mid), LANES - 1, 1)
            charge = charge_ref[z, rows_at, at]
            beside = z_low + z_high + mid + jnp.where(first_row, x_low, x_high) + y_low + y_high
            own = own_ref[z, rows_at, at]
            put(z, j, c, jnp.where(charge < PINNED, 0.25 * (beside + charge) - 0.5 * own, own))

    return tile_step


def line_scratch(planes, columns):
    return [pltpu.VMEM((planes // 2 * columns // LANES, LANES), jnp.float32)] * 2


def relax_kernel(colour, own_ref, other_ref, charge_ref, ze_ref, xo_ref, xe_ref, zi_ref, after,
                 out_ref, ze_out, xo_out, xe_out, zi_out, below, above):
    del after

    def put(z, j, c, value):
        out_ref[z, pl.ds(8 * j, 8), pl.ds(LANES * c, LANES)] = value

    step = relax(own_ref, other_ref, charge_ref, ze_ref, xo_ref, xe_ref, zi_ref, below, above, colour, put)
    for z in range(own_ref.shape[0]):
        for j in range(own_ref.shape[1] // 8):
            step(z, j)
    sends(out_ref, colour, *position()[:2], ze_out, xo_out, xe_out, zi_out)


def half_sweep(own, other, charge, halos, colour, after):
    return pl.pallas_call(
        functools.partial(relax_kernel, colour),
        in_specs=[vmem()] * 7 + [anywhere()],
        out_specs=[vmem()] * 5,
        out_shape=[shape_of(*own.shape)] + send_shapes(*own.shape),
        scratch_shapes=line_scratch(own.shape[0], own.shape[2]),
        compiler_params=params(),
        cost_estimate=cost(14 * own.size, 0),
        name="relax",
    )(own, other, charge, *halos, after)


def split(value):
    high = value.astype(jnp.bfloat16)
    return high, (value - high.astype(jnp.float32)).astype(jnp.bfloat16)


def angles_kernel(rows_total, tiles, columns, offset, after, left_ref, radial_ref, done_ref, terms_ref):
    del after
    done_ref[...] = jnp.zeros_like(done_ref)
    shape = (8, columns)
    column = lax.broadcasted_iota(jnp.int32, shape, 1)
    v = (column.astype(jnp.float32) + 0.5) * (2.0 / columns) - 1.0
    for j in range(tiles):
        packed = lax.broadcasted_iota(jnp.int32, shape, 0) * tiles + j
        row = lax.axis_index("gx") * (16 * tiles) + 2 * packed + (column + offset) % 2
        u = (row.astype(jnp.float32) + 0.5) * (2.0 / rows_total) - 1.0
        inverse = lax.rsqrt(u * u + v * v)
        c1, s1 = u * inverse, v * inverse
        c2, s2 = c1 * c1 - s1 * s1, 2.0 * (c1 * s1)
        c4, s4 = c2 * c2 - s2 * s2, 2.0 * (c2 * s2)
        u2, v2 = u * c1 - v * s1, u * s1 + v * c1
        u3, v3 = u2 * c1 - v2 * s1, u2 * s1 + v2 * c1
        u4, v4 = u2 * c2 - v2 * s2, u2 * s2 + v2 * c2
        for m, value in enumerate((u, u2, u3, u4, v, v2, v3, v4)):
            radial_ref[j, pl.ds(8 * m, 8), :] = value

        def put(index, pair):
            high, low = split(jnp.concatenate(pair, axis=0))
            terms_ref[pl.ds(8 * index, 16), :] = high
            terms_ref[pl.ds(8 * (2 * TURNS + index), 16), :] = low

        twice = 2.0 * c4
        cosines, sines = [jnp.ones_like(c4), c4], [jnp.zeros_like(c4), s4]
        for a in range(0, TURNS, 2):
            put(a, cosines)
            put(TURNS + a, sines)
            for terms in (cosines, sines):
                terms[0] = twice * terms[1] - terms[0]
                terms[1] = twice * terms[0] - terms[1]
        left_ref[j] = terms_ref[...].T


def angles(after, rows_total, tiles, columns, offset):
    left = jax.ShapeDtypeStruct((tiles, columns, 32 * TURNS), jnp.bfloat16)
    return pl.pallas_call(
        functools.partial(angles_kernel, rows_total, tiles, columns, offset),
        in_specs=[anywhere()],
        out_specs=[vmem()] * 3,
        out_shape=[left, shape_of(tiles, 16 * STEPS, columns), shape_of(8, LANES)],
        scratch_shapes=[pltpu.VMEM((32 * TURNS, columns), jnp.bfloat16)],
        compiler_params=params(),
        cost_estimate=cost(128 * tiles * 8 * columns, 0),
        name="angles",
    )(after)


def multipoles_of(colour, field_of, tables, planes, right):
    outs = [None] * planes
    pairs = planes // 2
    n, m = 16 * TURNS, 16 * STEPS * pairs
    tiles = tables[0][0].shape[0]
    totals = [None, None]

    def add_tile(e, j):
        left_ref, radial_ref = tables[e]
        slot = (e * tiles + j) % right.shape[0]
        for k in range(pairs):
            f = field_of(2 * k + (e + colour) % 2, j)
            twice = jnp.concatenate([f, f], axis=0)
            for b in range(0, 2 * STEPS, 2):
                high, low = split(twice * radial_ref[j, pl.ds(8 * b, 16), :])
                index = 2 * STEPS * k + b
                right[slot, pl.ds(8 * index, 16), :] = high
                right[slot, pl.ds(m + 8 * index, 16), :] = low
        product = jnp.dot(right[slot], left_ref[j], preferred_element_type=jnp.float32)
        totals[e] = product if totals[e] is None else totals[e] + product

    def finish():
        for e in (0, 1):
            total = totals[e]
            total = ((total[:m, :n] + total[m:, :n]) + (total[:m, n:] + total[m:, n:])).T
            i = lax.broadcasted_iota(jnp.int32, total.shape, 0)
            k = lax.broadcasted_iota(jnp.int32, total.shape, 1)
            total = jnp.sum(jnp.where(i % 8 == k % 8, total, 0.0).reshape(2 * TURNS, 8, m), axis=1)
            for shift in (1, 2, 4):
                total = total + pltpu.roll(total, shift, 1)
            half = 8 * STEPS
            even, odd = total[:TURNS], total[TURNS:]
            cosines = even - pltpu.roll(odd, m - half, 1)
            sines = odd + pltpu.roll(even, m - half, 1)
            lane = lax.broadcasted_iota(jnp.int32, (TURNS, m), 1)
            total = jnp.where(lane // half % 2 == 0, cosines, pltpu.roll(sines, half, 1))
            for k in range(pairs):
                outs[2 * k + (e + colour) % 2] = total[:, 2 * half * k : 2 * half * (k + 1)]
        return jnp.concatenate(outs, axis=1)

    return add_tile, finish


def right_scratch(planes, columns):
    return pltpu.VMEM((2, 16 * STEPS * planes, columns), jnp.bfloat16)


def sums_shape(planes):
    return shape_of(TURNS, 16 * STEPS * planes)


def multipole_kernel(field_ref, left0, radial0, left1, radial1, out_ref, done_ref, right):
    done_ref[...] = jnp.zeros_like(done_ref)
    planes, rows, _ = field_ref.shape
    add_tile, finish = multipoles_of(
        0, lambda z, j: field_ref[z, pl.ds(8 * j, 8), :], ((left0, radial0), (left1, radial1)), planes, right
    )
    for e in (0, 1):
        for j in range(rows // 8):
            add_tile(e, j)
    out_ref[...] = finish()


def multipole_sums(field, tables):
    planes, _, columns = field.shape
    return pl.pallas_call(
        multipole_kernel,
        in_specs=[vmem()] * 5,
        out_specs=[vmem()] * 2,
        out_shape=[sums_shape(planes), shape_of(8, LANES)],
        scratch_shapes=[right_scratch(planes, columns)],
        compiler_params=params(),
        cost_estimate=cost(100 * field.size, 0),
        name="multipole",
    )(field, *tables)


def last_kernel(scale, own_ref, other_ref, charge_ref, ze_ref, xo_ref, xe_ref, zi_ref, left0, radial0, left1,
                radial1, sums_ref, after, field_hbm, out_ref, one, staged, right, below, above, sems):
    del after
    planes, rows, columns = own_ref.shape
    tiles = rows // 8
    copies = []

    def put(z, j, c, value):
        at = pl.ds(LANES * c, LANES)
        one[z, pl.ds(8 * j, 8), at] = value
        even = column_parity(8, LANES) == z % 2
        zero = other_ref[z, pl.ds(8 * j, 8), at]
        staged[z, c, pl.ds(2 * j, 8, stride=2 * tiles), :] = jnp.where(even, zero, value)
        staged[z, c, pl.ds(2 * j + 1, 8, stride=2 * tiles), :] = jnp.where(even, value, zero)
        if j == tiles - 1:
            copy = pltpu.make_async_copy(staged.at[z, c], field_hbm.at[z, :, at], sems.at[z, c])
            copy.start()
            copies.append(copy)

    relax_tile = relax(own_ref, other_ref, charge_ref, ze_ref, xo_ref, xe_ref, zi_ref, below, above, 1, put)
    add_tile, finish = multipoles_of(
        1, lambda z, j: one[z, pl.ds(8 * j, 8), :], ((left0, radial0), (left1, radial1)), planes, right
    )
    for z in range(1, planes, 2):
        for j in range(tiles):
            relax_tile(z, j)
    for j in range(tiles):
        add_tile(0, j)
        for z in range(0, planes, 2):
            relax_tile(z, j)
    for j in range(tiles):
        add_tile(1, j)
    out_ref[...] = (finish() + sums_ref[...]) * scale
    for copy in copies:
        copy.wait()


def last_half_sweep(own, other, charge, halos, tables, sums, after, scale):
    planes, rows, columns = own.shape
    return pl.pallas_call(
        functools.partial(last_kernel, scale),
        in_specs=[vmem()] * 12 + [anywhere()],
        out_specs=[hbm(), vmem()],
        out_shape=[shape_of(planes, 2 * rows, columns), sums_shape(planes)],
        scratch_shapes=[
            pltpu.VMEM(own.shape, jnp.float32),
            pltpu.VMEM((planes, columns // LANES, 2 * rows, LANES), jnp.float32),
            right_scratch(planes, columns),
            *line_scratch(planes, columns),
            pltpu.SemaphoreType.DMA((planes, columns // LANES)),
        ],
        compiler_params=params(),
        cost_estimate=cost(100 * own.size, 0),
        name="relax_last",
    )(own, other, charge, *halos, *tables, sums, after)


def swaps(pairs):
    return [(a, b) for a, b in pairs] + [(b, a) for a, b in pairs]


def far_pairs(nx, nz):
    step = nx // 4
    pairs = [(x * nz + z, x * nz + z + 1) for x in range(nx) for z in range(1, nz - 1, 2)]
    ends = [x for x in range(nx) if x // step % 2 == 0]
    return swaps(pairs + [(x * nz + z, (x + step) * nz + z) for x in ends for z in (0, nz - 1)])


def odd_pairs(nx, nz):
    pairs = [(x * nz + z, (x + 1) * nz + z) for x in range(1, nx - 1, 2) for z in range(nz)]
    return swaps(pairs + [(x * nz + z, x * nz + z + 1) for x in (0, nx - 1) for z in range(0, nz, 2)])


def local(potential, regions, charge, levels):
    planes, row_count, columns = potential.shape
    nx, nz = lax.axis_size("gx"), lax.axis_size("gz")
    rows_total = nx * row_count
    tiles = row_count // 16
    z_near, x_even = [(i, i ^ 1) for i in range(nz)], [(i, i ^ 1) for i in range(nx)]
    z_far, x_odd = far_pairs(nx, nz), odd_pairs(nx, nz)

    def exchange(ze, xo, xe, zi):
        ze = lax.ppermute(ze, ("gx", "gz"), z_far)
        xo = lax.ppermute(xo, ("gx", "gz"), x_odd)
        xe = lax.ppermute(xe, "gx", x_even)
        zi = lax.ppermute(zi, "gz", z_near)
        return ze, xo, xe, zi

    *packed, ze, xo, xe, zi = pack(potential, regions, levels)
    out = ze, xo, xe, zi
    zero, one, charge0, charge1, after = pack_rest(potential, regions, charge, levels, packed, xo)
    tables = []
    for sweep in range(SWEEPS):
        halos = exchange(*out)
        zero, *out = half_sweep(zero, one, charge0, halos, 0, after)
        halos = exchange(*out)
        after = zero
        if sweep < SWEEPS - 1:
            if sweep < 2:
                *table, after = angles(out[1], rows_total, tiles, columns, sweep)
                tables += table
            one, *out = half_sweep(one, zero, charge1, halos, 1, after)
            after = one
    sums, after = multipole_sums(zero, tables)
    scale = 1.0 / math.sqrt(rows_total * columns)
    field, sums = last_half_sweep(one, zero, charge1, halos, tables, sums, after, scale)
    share = K // nx
    parts = jnp.transpose(sums[:, 7::8].reshape(TURNS, planes, 2, STEPS), (2, 0, 3, 1)).reshape(nx, share * planes)
    shares = lax.all_to_all(parts, "gx", 0, 0, tiled=True)
    return field, jnp.sum(shares, axis=0).reshape(share, planes).T


def solution(mesh):
    in_specs = (P("gz", "gx", None), P("gz", "gx", None), P("gz", "gx", None), P())
    out_specs = (P("gz", "gx", None), P("gz", "gx"))
    return jax.shard_map(local, mesh=mesh, in_specs=in_specs, out_specs=out_specs, check_vma=False)
```
